32 devices in a mesh: row: 4 (over y, x), col: 8 (over z, core).
Axes of the slice: x: 2, y: 2, z: 4, core: 2. Of those that a mesh axis runs over, the one named last changes fastest.
Arguments:
- gradients: bfloat16 [3, 32, 512, 512], P(None, None, ('row', 'col')), may hold values from -6 to 6
- factors: float32 [2, 32, 512, 512], P(None, None, ('row', 'col')), as said below
- slot_block: int32 [32], replicated, may hold values from 0 to 31, each once
- layer_of_block: int32 [32], replicated, may hold values from 0 to 3
- layer_step_scale: float32 [4], replicated, may hold values from 0.25 to 4
Outputs:
- new_factors: float32 [2, 32, 512, 512], P(None, ('row', 'col'))
- update: bfloat16 [32, 512, 512], P(None, ('row', 'col'))
The draws below stay inside these ranges and needn't reach their ends.
Inputs may be any that keep to these rules, and one draw needn't show every extreme that they name: Every block factors[i, b] is symmetric positive definite with eigenvalues of 0.25 or more. `slot_block`: each block number stands in exactly one slot; slot j belongs to owner device j in the order of row+col (one slot per device).
All inputs are finite; a program needn't handle non-finite values.
Results may differ from the reference program's by a relative error of at most 0.0069.
Values may be sent and summed in bfloat16 or wider, within the bound.
A program may use at most 64 MiB of HBM per device.

```python
import math
import jax
import jax.numpy as jnp
from jax import lax

BS = 512
STEPS = 3
ITERS = 6
LAYERS = 4
NB = 32


def draw_factors(key, part):
    key_list = jax.random.split(jax.random.fold_in(key, 7), 2 * NB)

    def single(one_key):
        first_key = jax.random.fold_in(one_key, 1)
        second_key = jax.random.fold_in(one_key, 2)
        mixing = jax.random.normal(first_key, (BS, BS), jnp.float32)
        spread = jnp.exp(jax.random.uniform(second_key, (BS,), jnp.float32, 0.0, math.log(3.0)))
        inner_part = jnp.dot(mixing, mixing.T, precision=lax.Precision.HIGHEST) / BS + 0.25 * jnp.eye(BS, dtype=jnp.float32)
        return inner_part * spread[:, None] * spread[None, :]
    blocks = lax.map(single, key_list)
    return blocks.reshape(2, NB, BS, BS)


def plant(array, rng, least, largest):
    longest = array.shape.index(max(array.shape))
    spots = []
    for shift in (0, 1):
        where = [jax.random.randint(jax.random.fold_in(rng, axis), (), 0, length) for axis, length in enumerate(array.shape)]
        where[longest] = (where[longest] + shift) % array.shape[longest]
        spots.append(tuple(where))
    return array.at[spots[0]].set(least).at[spots[1]].set(largest)


def level_of(rng, dims, pieces, smallest, high):
    factor_of, own = 1.0, jax.random.fold_in(rng, 6)
    for axis_at, shards_of in pieces:
        steps = jnp.exp(jax.random.uniform(jax.random.fold_in(own, axis_at), (shards_of,), jnp.float32, smallest / len(pieces), high / len(pieces)))
        factor_of = factor_of * jnp.repeat(steps, dims[axis_at] // shards_of).reshape([-1 if axis == axis_at else 1 for axis in range(len(dims))])
    return factor_of


def gaussian(key, dims, width, limit, shards=(), kind=jnp.bfloat16):
    factor_of = level_of(key, dims, shards, -0.22, 0.18) if shards else 1.0
    entries = jax.random.normal(key, dims, jnp.float32) * width * factor_of
    return jnp.minimum(jnp.maximum(entries, -limit), limit).astype(kind)


def setup_inputs(seed: int = 0) -> dict:
    key_of = jax.random.split(jax.random.key(seed), 6)
    gradients = gaussian(key_of[0], (STEPS, NB, BS, BS), 1.0, 6.0, ((2, 32),))
    factors = draw_factors(jax.random.fold_in(key_of[5], 71), 0)
    slot_block = jax.random.permutation(key_of[2], NB).astype(jnp.int32)
    layer_of_block = plant(jax.random.randint(key_of[3], (NB,), 0, LAYERS), jax.random.fold_in(key_of[3], 1), 0, LAYERS - 1).astype(jnp.int32)
    layer_step_scale = jnp.clip(jnp.exp(jax.random.uniform(key_of[4], (LAYERS,), jnp.float32, math.log(0.25), math.log(4.0))), 0.25, 4.0)
    return {"gradients": gradients, "factors": factors, "slot_block": slot_block, "layer_of_block": layer_of_block, "layer_step_scale": layer_step_scale}


def inverse_root(matrix):
    unit_matrix = jnp.eye(matrix.shape[0], dtype=jnp.float32)
    frobenius = jnp.sqrt(jnp.sum(matrix * matrix))
    mixer = matrix / frobenius
    approx = unit_matrix * frobenius ** (-0.25)
    for newton_sweep in range(ITERS):
        factor_p = (5.0 * unit_matrix - mixer) * 0.25
        approx = jnp.dot(approx, factor_p, precision=lax.Precision.HIGHEST)
        second_root_factor = jnp.dot(factor_p, factor_p, precision=lax.Precision.HIGHEST)
        mixer = jnp.dot(second_root_factor, jnp.dot(second_root_factor, mixer, precision=lax.Precision.HIGHEST), precision=lax.Precision.HIGHEST)
    return approx

def reference(gradients, factors, slot_block, layer_of_block, layer_step_scale):

    def per_slot(slot):
        block = slot_block[slot]
        gradient = lax.dynamic_index_in_dim(gradients, block, 1, keepdims=False)
        held = lax.dynamic_index_in_dim(factors, block, 1, keepdims=False)
        gram_left = jnp.zeros((BS, BS), jnp.float32)
        gram_right = jnp.zeros((BS, BS), jnp.float32)
        for moment in range(STEPS):
            gram_left = gram_left + jnp.dot(gradient[moment], gradient[moment].T, preferred_element_type=jnp.float32)
            gram_right = gram_right + jnp.dot(gradient[moment].T, gradient[moment], preferred_element_type=jnp.float32)
        left_stat = held[0] + gram_left / BS
        right_stat = held[1] + gram_right / BS
        root_left_half = inverse_root(left_stat).astype(jnp.bfloat16)
        root_right_half = inverse_root(right_stat).astype(jnp.bfloat16)
        step_multiplier = layer_step_scale[layer_of_block[block]]
        left_applied = jnp.dot(root_left_half, gradient[STEPS - 1], preferred_element_type=jnp.float32).astype(jnp.bfloat16)
        product = jnp.dot(left_applied, root_right_half, preferred_element_type=jnp.float32)
        return (left_stat, right_stat, (step_multiplier * product).astype(jnp.bfloat16))
    lefts, rights, moved = lax.map(per_slot, jnp.arange(NB, dtype=jnp.int32))
    new_factors = jnp.stack([lefts, rights])
    update = jnp.zeros_like(moved).at[slot_block].set(moved)
    return (new_factors, update)
```

```python
import functools

import jax
import jax.numpy as jnp
from jax import lax
from jax.experimental import pallas as pl
from jax.experimental.pallas import tpu as pltpu
from jax.sharding import PartitionSpec as P

MESH = pl.DeviceIdType.MESH
SWITCH = 4

ITERS = 6


def inverse_root(matrix):
    unit_matrix = jnp.eye(matrix.shape[0], dtype=jnp.float32)
    frobenius = jnp.sqrt(jnp.sum(matrix * matrix))
    mixer = matrix / frobenius
    approx = unit_matrix * frobenius ** (-0.25)
    for newton_sweep in range(ITERS):
        factor_p = (5.0 * unit_matrix - mixer) * 0.25
        approx = jnp.dot(approx, factor_p, precision=lax.Precision.HIGHEST)
        second_root_factor = jnp.dot(factor_p, factor_p, precision=lax.Precision.HIGHEST)
        mixer = jnp.dot(
            second_root_factor,
            jnp.dot(second_root_factor, mixer, precision=lax.Precision.HIGHEST),
            precision=lax.Precision.HIGHEST,
        )
    return approx


def plain_body(gradients, factors, slot_block, layer_of_block, layer_step_scale):
    count_steps, block_count, row_slab, block_side = gradients.shape
    row_count = lax.axis_size("row")
    col_count = lax.axis_size("col")
    devices_all = row_count * col_count
    per_device = block_count // devices_all
    ordered_grads = jnp.take(gradients, slot_block, axis=1)
    ordered_factors = jnp.take(factors, slot_block, axis=1)
    owned_grads = lax.all_to_all(
        ordered_grads.reshape(count_steps, block_count, 1, row_slab, block_side),
        ("row", "col"),
        split_axis=1,
        concat_axis=2,
        tiled=True,
    )
    owned_factors = lax.all_to_all(
        ordered_factors.reshape(2, block_count, 1, row_slab, block_side),
        ("row", "col"),
        split_axis=1,
        concat_axis=2,
        tiled=True,
    )
    owned_grads = owned_grads.reshape(count_steps, per_device, block_side, block_side)
    owned_factors = owned_factors.reshape(2, per_device, block_side, block_side)
    first_slot = (lax.axis_index("row") * col_count + lax.axis_index("col")) * per_device
    own_slots = first_slot + jnp.arange(per_device, dtype=jnp.int32)
    own_blocks = jnp.take(slot_block, own_slots)
    own_layers = jnp.take(layer_of_block, own_blocks)
    layer_hits = (
        own_layers[:, None] == jnp.arange(layer_step_scale.shape[0], dtype=jnp.int32)[None, :]
    )
    step_multipliers = jnp.sum(jnp.where(layer_hits, layer_step_scale[None, :], 0.0), axis=1)

    def per_slot(block_position):
        gradient = lax.dynamic_index_in_dim(owned_grads, block_position, 1, keepdims=False)
        held = lax.dynamic_index_in_dim(owned_factors, block_position, 1, keepdims=False)
        gram_left = jnp.einsum(
            "sik,sjk->ij", gradient, gradient, preferred_element_type=jnp.float32
        )
        gram_right = jnp.einsum(
            "ski,skj->ij", gradient, gradient, preferred_element_type=jnp.float32
        )
        left_stat = held[0] + gram_left / block_side
        right_stat = held[1] + gram_right / block_side
        root_left_half = inverse_root(left_stat).astype(jnp.bfloat16)
        root_right_half = inverse_root(right_stat).astype(jnp.bfloat16)
        step_multiplier = lax.dynamic_index_in_dim(
            step_multipliers, block_position, 0, keepdims=False
        )
        left_applied = jnp.dot(
            root_left_half, gradient[count_steps - 1], preferred_element_type=jnp.float32
        ).astype(jnp.bfloat16)
        product = jnp.dot(left_applied, root_right_half, preferred_element_type=jnp.float32)
        return (left_stat, right_stat, (step_multiplier * product).astype(jnp.bfloat16))

    lefts, rights, moved = lax.map(per_slot, jnp.arange(per_device, dtype=jnp.int32))
    new_factors = jnp.stack([lefts, rights])
    returned = lax.all_to_all(
        moved.reshape(1, 1, per_device, devices_all, row_slab, block_side),
        ("row", "col"),
        split_axis=3,
        concat_axis=1,
        tiled=True,
    )
    returned = returned.reshape(block_count, row_slab, block_side)
    update = jnp.zeros_like(returned).at[slot_block].set(returned)
    return (new_factors, update)


def dot(a, b, contract=((1,), (0,))):
    return lax.dot_general(
        a.astype(jnp.bfloat16),
        b.astype(jnp.bfloat16),
        (contract, ((), ())),
        preferred_element_type=jnp.float32,
    )


def fused_kernel(
    rows_of,
    cols_of,
    slot_ref,
    inverse_ref,
    layer_ref,
    scale_ref,
    g_ref,
    f_ref,
    nf_ref,
    upd_ref,
    staged_g,
    staged_f,
    staged_x,
    grads,
    facts,
    cross,
    acc,
    turned,
    mixer,
    approx,
    applied,
    moved,
    returned,
    g_send,
    g_recv,
    f_send,
    f_recv,
    u_send,
    u_recv,
):
    steps, blocks, slab, side = g_ref.shape
    half_cols = cols_of // 2
    chunk = slab * half_cols
    half_side = side // 2
    row = lax.axis_index("row")
    col = lax.axis_index("col")
    me = row * cols_of + col
    half = col // half_cols
    place = col % half_cols

    def strip(index):
        return pl.ds(pl.multiple_of(index * slab, slab), slab)

    def same_half(k):
        return (row + k // half_cols) % rows_of, half * half_cols + (place + k % half_cols) % half_cols

    def other_half(k):
        return (
            (row + k // half_cols) % rows_of,
            (1 - half) * half_cols + (place + k % half_cols) % half_cols,
        )

    pairs = rows_of * half_cols

    barrier = pltpu.get_barrier_semaphore()

    def greet(k, carry):
        @pl.when(k > 0)
        def _():
            pl.semaphore_signal(barrier, inc=1, device_id=same_half(k), device_id_type=MESH)

        pl.semaphore_signal(barrier, inc=1, device_id=other_half(k), device_id_type=MESH)
        return carry

    lax.fori_loop(0, pairs, greet, 0)

    def stage_gradients(slot, carry):
        for step in range(steps):
            staged_g[step, strip(slot), :] = g_ref[step, slot_ref[slot]]
        return carry

    lax.fori_loop(0, blocks, stage_gradients, 0)
    pl.semaphore_wait(barrier, blocks - 1)

    def send_gradients(step):
        def ship(peer):
            target = peer[0] * cols_of + peer[1]
            pltpu.make_async_remote_copy(
                src_ref=staged_g.at[step, strip(target), :],
                dst_ref=grads.at[step, strip(me), :],
                send_sem=g_send.at[step],
                recv_sem=g_recv.at[step],
                device_id=peer,
                device_id_type=MESH,
            ).start()

        def one(k, carry):
            ship(other_half(k))

            @pl.when(k > 0)
            def _():
                ship(same_half(k))

            return carry

        lax.fori_loop(0, pairs, one, 0)
        pltpu.make_async_copy(
            staged_g.at[step, strip(me), :], grads.at[step, strip(me), :], g_recv.at[step]
        ).start()

    send_gradients(0)

    def stage_statistics(slot, carry):
        for which in range(2):
            staged_f[which, strip(slot), :] = f_ref[which, slot_ref[slot]].astype(jnp.bfloat16)
        return carry

    lax.fori_loop(0, blocks, stage_statistics, 0)
    natural = lax.broadcasted_iota(jnp.int32, (side, half_side), 0)
    packed = lax.broadcasted_iota(jnp.int32, (side, half_side), 1)
    doubled = 2 * packed - (packed & (chunk - 1))
    pick = jnp.where(natural == doubled + half * chunk, 1.0, 0.0).astype(jnp.bfloat16)
    for which in range(2):
        staged_x[which] = dot(staged_f[which], pick).astype(jnp.bfloat16)

    def send_statistics(k, carry):
        far = other_half(k)
        pltpu.make_async_remote_copy(
            src_ref=staged_x.at[:, strip(far[0] * cols_of + far[1]), :],
            dst_ref=cross.at[:, strip(me), :],
            send_sem=f_send.at[1],
            recv_sem=f_recv.at[1],
            device_id=far,
            device_id_type=MESH,
        ).start()

        @pl.when(k > 0)
        def _():
            near = same_half(k)
            pltpu.make_async_remote_copy(
                src_ref=staged_f.at[:, strip(near[0] * cols_of + near[1]), :],
                dst_ref=facts.at[:, strip(me), :],
                send_sem=f_send.at[0],
                recv_sem=f_recv.at[0],
                device_id=near,
                device_id_type=MESH,
            ).start()

        return carry

    lax.fori_loop(0, pairs, send_statistics, 0)
    pltpu.make_async_copy(
        staged_f.at[:, strip(me), :], facts.at[:, strip(me), :], f_recv.at[0]
    ).start()
    for step in range(1, steps):
        send_gradients(step)

    def wait_gradients(step):
        pltpu.make_async_copy(staged_g.at[step], grads.at[step], g_recv.at[step]).wait()

    def add_gram(step):
        held = grads[step]
        left = dot(held, held, ((1,), (1,)))
        right = dot(held, held, ((0,), (0,)))
        if step == 0:
            acc[0] = left
            acc[1] = right
        else:
            acc[0] += left
            acc[1] += right

    wait_gradients(0)
    add_gram(0)

    pltpu.make_async_copy(
        staged_f.at[:, pl.ds(0, half_side), :], facts.at[:, pl.ds(0, half_side), :], f_recv.at[0]
    ).wait()
    pltpu.make_async_copy(
        staged_x.at[:, pl.ds(0, half_side), :], cross.at[:, pl.ds(0, half_side), :], f_recv.at[1]
    ).wait()
    wide_packed = lax.broadcasted_iota(jnp.int32, (half_side, side), 0)
    wide_natural = lax.broadcasted_iota(jnp.int32, (half_side, side), 1)
    spread = jnp.where(
        wide_natural == 2 * wide_packed - (wide_packed & (chunk - 1)) + (1 - half) * chunk, 1.0, 0.0
    ).astype(jnp.bfloat16)
    lane = lax.broadcasted_iota(jnp.int32, (chunk, side), 1)
    mine = (lane & chunk) == half * chunk
    for which in range(2):
        turned[...] = facts[which].astype(jnp.float32).T
        for part in range(rows_of):
            own = pl.ds(pl.multiple_of(part * 2 * chunk + half * chunk, chunk), chunk)
            rest = pl.ds(pl.multiple_of(part * 2 * chunk + (1 - half) * chunk, chunk), chunk)
            nf_ref[which, 0, own, :] = facts[which, own, :].astype(jnp.float32)
            far = dot(cross[which, rest, :], spread)
            nf_ref[which, 0, rest, :] = jnp.where(mine, turned[rest, :], far)

    for step in range(1, steps):
        wait_gradients(step)
        add_gram(step)

    eye = (
        lax.broadcasted_iota(jnp.int32, (side, side), 0)
        == lax.broadcasted_iota(jnp.int32, (side, side), 1)
    )
    unit = jnp.where(eye, 1.0, 0.0).astype(jnp.float32)
    for which in range(2):
        stat = nf_ref[which, 0] + acc[which] / side
        nf_ref[which, 0] = stat
        total = jnp.sum(jnp.sum(stat * stat, axis=0, keepdims=True), axis=1, keepdims=True)
        frobenius = jnp.sqrt(total)
        start = 1.0 / jnp.sqrt(jnp.sqrt(frobenius))
        mixer[which] = stat / frobenius
        approx[which] = start * (1.25 * unit - 0.25 * mixer[which])

    def grow(which):
        m = mixer[which]
        lead = (dot(m, m) - 10.0 * m) * 0.0625
        inner = 1.5625 * m + dot(lead, m)
        return 1.5625 * inner + dot(lead, inner)

    for sweep in range(SWITCH):
        for which in range(2):
            if sweep > 0:
                x = approx[which]
                approx[which] = 1.25 * x - 0.25 * dot(x, mixer[which])
            grown = grow(which)
            mixer[which] = grown - unit if sweep == SWITCH - 1 else grown
    for sweep in range(SWITCH, ITERS):
        for which in range(2):
            x, e = approx[which], mixer[which]
            approx[which] = x - 0.25 * dot(x, e)
            if sweep < ITERS - 1:
                lead = 0.0625 * dot(e, e) - 0.5 * e
                inner = lead + e + dot(lead, e)
                mixer[which] = lead + inner + dot(lead, inner)

    multiplier = scale_ref[layer_ref[slot_ref[me]]]
    applied[...] = dot(approx[0], grads[steps - 1]).astype(jnp.bfloat16)
    right_half = approx[1].astype(jnp.bfloat16)
    band = slab * cols_of
    for turn in range(rows_of):
        target_row = (row + turn) % rows_of
        rows = pl.ds(pl.multiple_of(target_row * band, band), band)
        moved[rows, :] = (multiplier * dot(applied[rows, :], right_half)).astype(jnp.bfloat16)

        def give_back(k, carry):
            target_col = (col + 3 * k) % cols_of
            target = target_row * cols_of + target_col
            pltpu.make_async_remote_copy(
                src_ref=moved.at[strip(target), :],
                dst_ref=returned.at[me],
                send_sem=u_send,
                recv_sem=u_recv,
                device_id=(target_row, target_col),
                device_id_type=MESH,
            ).start()
            return carry

        lax.fori_loop(1 if turn == 0 else 0, cols_of, give_back, 0)
    pltpu.make_async_copy(moved.at[strip(me), :], returned.at[me], u_recv).start()

    most = side - slab
    for step in range(steps):
        sent = staged_g.at[step, pl.ds(0, most), :]
        pltpu.make_async_copy(sent, sent, g_send.at[step]).wait()
    near = staged_f.at[:, pl.ds(0, half_side - slab), :]
    pltpu.make_async_copy(near, near, f_send.at[0]).wait()
    far = staged_x.at[:, pl.ds(0, half_side), :]
    pltpu.make_async_copy(far, far, f_send.at[1]).wait()
    pltpu.make_async_copy(returned, returned, u_recv).wait()

    def unpack(block, carry):
        upd_ref[block] = returned[inverse_ref[block]]
        return carry

    lax.fori_loop(0, blocks, unpack, 0)
    pltpu.make_async_copy(
        moved.at[pl.ds(0, most), :], moved.at[pl.ds(0, most), :], u_send
    ).wait()


def fused_body(rows_of, cols_of, gradients, factors, slot_block, layer_of_block, layer_step_scale):
    steps, blocks, slab, side = gradients.shape
    half_side = side // 2
    in_vmem = pl.BlockSpec(memory_space=pltpu.VMEM)
    in_smem = pl.BlockSpec(memory_space=pltpu.SMEM)
    bf16, f32 = jnp.bfloat16, jnp.float32
    order = jnp.arange(blocks, dtype=jnp.int32)
    inverse = jnp.sum(jnp.where(slot_block[None, :] == order[:, None], order[None, :], 0), axis=1)
    return pl.pallas_call(
        functools.partial(fused_kernel, rows_of, cols_of),
        out_shape=(
            jax.ShapeDtypeStruct((2, 1, side, side), f32),
            jax.ShapeDtypeStruct((blocks, slab, side), bf16),
        ),
        in_specs=[in_smem] * 4 + [in_vmem] * 2,
        out_specs=(in_vmem, in_vmem),
        scratch_shapes=[
            pltpu.VMEM((steps, side, side), bf16),
            pltpu.VMEM((2, side, side), bf16),
            pltpu.VMEM((2, side, half_side), bf16),
            pltpu.VMEM((steps, side, side), bf16),
            pltpu.VMEM((2, side, side), bf16),
            pltpu.VMEM((2, side, half_side), bf16),
            pltpu.VMEM((2, side, side), f32),
            pltpu.VMEM((side, side), f32),
            pltpu.VMEM((2, side, side), f32),
            pltpu.VMEM((2, side, side), f32),
            pltpu.VMEM((side, side), bf16),
            pltpu.VMEM((side, side), bf16),
            pltpu.VMEM((blocks, slab, side), bf16),
            pltpu.SemaphoreType.DMA((steps,)),
            pltpu.SemaphoreType.DMA((steps,)),
            pltpu.SemaphoreType.DMA((2,)),
            pltpu.SemaphoreType.DMA((2,)),
            pltpu.SemaphoreType.DMA,
            pltpu.SemaphoreType.DMA,
        ],
        compiler_params=pltpu.CompilerParams(
            collective_id=0, has_side_effects=True, vmem_limit_bytes=56 * 1024 * 1024
        ),
    )(slot_block, inverse, layer_of_block, layer_step_scale, gradients, factors)


def fits(rows_of, cols_of, blocks, slab, side):
    chunk = slab * cols_of // 2
    return (
        blocks == rows_of * cols_of
        and slab % 16 == 0
        and cols_of % 2 == 0
        and cols_of % 3 != 0
        and chunk & (chunk - 1) == 0
        and side % 256 == 0
    )


def solution(mesh):
    rows_of, cols_of = mesh.shape["row"], mesh.shape["col"]

    def body(gradients, factors, *rest):
        _, blocks, slab, side = gradients.shape
        if fits(rows_of, cols_of, blocks, slab, side):
            return fused_body(rows_of, cols_of, gradients, factors, *rest)
        return plain_body(gradients, factors, *rest)

    return jax.shard_map(
        body,
        mesh=mesh,
        in_specs=(
            P(None, None, ("row", "col"), None),
            P(None, None, ("row", "col"), None),
            P(),
            P(),
            P(),
        ),
        out_specs=(P(None, ("row", "col"), None, None), P(None, ("row", "col"), None)),
        check_vma=False,
    )
```

```python
import functools

import jax
import jax.numpy as jnp
from jax import lax
from jax.experimental import pallas as pl
from jax.experimental.pallas import tpu as pltpu
from jax.sharding import PartitionSpec as P

MESH = pl.DeviceIdType.MESH
SWITCH = 4

ITERS = 6


def inverse_root(matrix):
    unit_matrix = jnp.eye(matrix.shape[0], dtype=jnp.float32)
    frobenius = jnp.sqrt(jnp.sum(matrix * matrix))
    mixer = matrix / frobenius
    approx = unit_matrix * frobenius ** (-0.25)
    for newton_sweep in range(ITERS):
        factor_p = (5.0 * unit_matrix - mixer) * 0.25
        approx = jnp.dot(approx, factor_p, precision=lax.Precision.HIGHEST)
        second_root_factor = jnp.dot(factor_p, factor_p, precision=lax.Precision.HIGHEST)
        mixer = jnp.dot(
            second_root_factor,
            jnp.dot(second_root_factor, mixer, precision=lax.Precision.HIGHEST),
            precision=lax.Precision.HIGHEST,
        )
    return approx


def plain_body(gradients, factors, slot_block, layer_of_block, layer_step_scale):
    count_steps, block_count, row_slab, block_side = gradients.shape
    row_count = lax.axis_size("row")
    col_count = lax.axis_size("col")
    devices_all = row_count * col_count
    per_device = block_count // devices_all
    ordered_grads = jnp.take(gradients, slot_block, axis=1)
    ordered_factors = jnp.take(factors, slot_block, axis=1)
    owned_grads = lax.all_to_all(
        ordered_grads.reshape(count_steps, block_count, 1, row_slab, block_side),
        ("row", "col"),
        split_axis=1,
        concat_axis=2,
        tiled=True,
    )
    owned_factors = lax.all_to_all(
        ordered_factors.reshape(2, block_count, 1, row_slab, block_side),
        ("row", "col"),
        split_axis=1,
        concat_axis=2,
        tiled=True,
    )
    owned_grads = owned_grads.reshape(count_steps, per_device, block_side, block_side)
    owned_factors = owned_factors.reshape(2, per_device, block_side, block_side)
    first_slot = (lax.axis_index("row") * col_count + lax.axis_index("col")) * per_device
    own_slots = first_slot + jnp.arange(per_device, dtype=jnp.int32)
    own_blocks = jnp.take(slot_block, own_slots)
    own_layers = jnp.take(layer_of_block, own_blocks)
    layer_hits = (
        own_layers[:, None] == jnp.arange(layer_step_scale.shape[0], dtype=jnp.int32)[None, :]
    )
    step_multipliers = jnp.sum(jnp.where(layer_hits, layer_step_scale[None, :], 0.0), axis=1)

    def per_slot(block_position):
        gradient = lax.dynamic_index_in_dim(owned_grads, block_position, 1, keepdims=False)
        held = lax.dynamic_index_in_dim(owned_factors, block_position, 1, keepdims=False)
        gram_left = jnp.einsum(
            "sik,sjk->ij", gradient, gradient, preferred_element_type=jnp.float32
        )
        gram_right = jnp.einsum(
            "ski,skj->ij", gradient, gradient, preferred_element_type=jnp.float32
        )
        left_stat = held[0] + gram_left / block_side
        right_stat = held[1] + gram_right / block_side
        root_left_half = inverse_root(left_stat).astype(jnp.bfloat16)
        root_right_half = inverse_root(right_stat).astype(jnp.bfloat16)
        step_multiplier = lax.dynamic_index_in_dim(
            step_multipliers, block_position, 0, keepdims=False
        )
        left_applied = jnp.dot(
            root_left_half, gradient[count_steps - 1], preferred_element_type=jnp.float32
        ).astype(jnp.bfloat16)
        product = jnp.dot(left_applied, root_right_half, preferred_element_type=jnp.float32)
        return (left_stat, right_stat, (step_multiplier * product).astype(jnp.bfloat16))

    lefts, rights, moved = lax.map(per_slot, jnp.arange(per_device, dtype=jnp.int32))
    new_factors = jnp.stack([lefts, rights])
    returned = lax.all_to_all(
        moved.reshape(1, 1, per_device, devices_all, row_slab, block_side),
        ("row", "col"),
        split_axis=3,
        concat_axis=1,
        tiled=True,
    )
    returned = returned.reshape(block_count, row_slab, block_side)
    update = jnp.zeros_like(returned).at[slot_block].set(returned)
    return (new_factors, update)


def dot(a, b, contract=((1,), (0,))):
    return lax.dot_general(
        a.astype(jnp.bfloat16),
        b.astype(jnp.bfloat16),
        (contract, ((), ())),
        preferred_element_type=jnp.float32,
    )


def fused_kernel(
    rows_of,
    cols_of,
    slot_ref,
    inverse_ref,
    layer_ref,
    scale_ref,
    g_far,
    f_far,
    nf_ref,
    upd_ref,
    g_ref,
    f_ref,
    staged_g,
    staged_f,
    staged_x,
    grads,
    facts,
    cross,
    acc,
    turned,
    mixer,
    approx,
    applied,
    moved,
    returned,
    g_send,
    g_recv,
    f_send,
    f_recv,
    u_send,
    u_recv,
    in_sem,
):
    steps, blocks, slab, side = g_ref.shape
    half_cols = cols_of // 2
    chunk = slab * half_cols
    half_side = side // 2
    row = lax.axis_index("row")
    col = lax.axis_index("col")
    me = row * cols_of + col
    half = col // half_cols
    place = col % half_cols

    def strip(index):
        return pl.ds(pl.multiple_of(index * slab, slab), slab)

    def same_half(k):
        return (row + k // half_cols) % rows_of, half * half_cols + (place + k % half_cols) % half_cols

    def other_half(k):
        return (
            (row + k // half_cols) % rows_of,
            (1 - half) * half_cols + (place + k % half_cols) % half_cols,
        )

    pairs = rows_of * half_cols
    g_fetch = pltpu.make_async_copy(g_far, g_ref, in_sem.at[0])
    f_fetch = pltpu.make_async_copy(f_far, f_ref, in_sem.at[1])
    g_fetch.start()
    f_fetch.start()

    barrier = pltpu.get_barrier_semaphore()

    def greet(k, carry):
        @pl.when(k > 0)
        def _():
            pl.semaphore_signal(barrier, inc=1, device_id=same_half(k), device_id_type=MESH)

        pl.semaphore_signal(barrier, inc=1, device_id=other_half(k), device_id_type=MESH)
        return carry

    lax.fori_loop(0, pairs, greet, 0)

    def stage_gradients(step):
        def one(slot, carry):
            staged_g[step, strip(slot), :] = g_ref[step, slot_ref[slot]]
            return carry

        lax.fori_loop(0, blocks, one, 0, unroll=4)

    g_fetch.wait()
    stage_gradients(0)
    pl.semaphore_wait(barrier, blocks - 1)

    def send_gradients(step):
        def ship(peer):
            target = peer[0] * cols_of + peer[1]
            pltpu.make_async_remote_copy(
                src_ref=staged_g.at[step, strip(target), :],
                dst_ref=grads.at[step, strip(me), :],
                send_sem=g_send.at[step],
                recv_sem=g_recv.at[step],
                device_id=peer,
                device_id_type=MESH,
            ).start()

        def one(k, carry):
            ship(other_half(k))

            @pl.when(k > 0)
            def _():
                ship(same_half(k))

            return carry

        lax.fori_loop(0, pairs, one, 0)
        pltpu.make_async_copy(
            staged_g.at[step, strip(me), :], grads.at[step, strip(me), :], g_recv.at[step]
        ).start()

    send_gradients(0)

    def stage_statistics(slot, carry):
        for which in range(2):
            staged_f[which, strip(slot), :] = f_ref[which, slot_ref[slot]].astype(jnp.bfloat16)
        return carry

    f_fetch.wait()
    lax.fori_loop(0, blocks, stage_statistics, 0, unroll=2)
    natural = lax.broadcasted_iota(jnp.int32, (side, half_side), 0)
    packed = lax.broadcasted_iota(jnp.int32, (side, half_side), 1)
    doubled = 2 * packed - (packed & (chunk - 1))
    pick = jnp.where(natural == doubled + half * chunk, 1.0, 0.0).astype(jnp.bfloat16)
    for which in range(2):
        staged_x[which] = dot(staged_f[which], pick).astype(jnp.bfloat16)

    def send_statistics(k, carry):
        far = other_half(k)
        pltpu.make_async_remote_copy(
            src_ref=staged_x.at[:, strip(far[0] * cols_of + far[1]), :],
            dst_ref=cross.at[:, strip(me), :],
            send_sem=f_send.at[1],
            recv_sem=f_recv.at[1],
            device_id=far,
            device_id_type=MESH,
        ).start()

        @pl.when(k > 0)
        def _():
            near = same_half(k)
            pltpu.make_async_remote_copy(
                src_ref=staged_f.at[:, strip(near[0] * cols_of + near[1]), :],
                dst_ref=facts.at[:, strip(me), :],
                send_sem=f_send.at[0],
                recv_sem=f_recv.at[0],
                device_id=near,
                device_id_type=MESH,
            ).start()

        return carry

    lax.fori_loop(0, pairs, send_statistics, 0)
    pltpu.make_async_copy(
        staged_f.at[:, strip(me), :], facts.at[:, strip(me), :], f_recv.at[0]
    ).start()
    for step in range(1, steps):
        stage_gradients(step)
        send_gradients(step)

    def wait_gradients(step):
        pltpu.make_async_copy(staged_g.at[step], grads.at[step], g_recv.at[step]).wait()

    def add_gram(step):
        held = grads[step]
        left = dot(held, held, ((1,), (1,)))
        right = dot(held, held, ((0,), (0,)))
        if step == 0:
            acc[0] = left
            acc[1] = right
        else:
            acc[0] += left
            acc[1] += right

    wait_gradients(0)
    add_gram(0)

    pltpu.make_async_copy(
        staged_f.at[:, pl.ds(0, half_side), :], facts.at[:, pl.ds(0, half_side), :], f_recv.at[0]
    ).wait()
    pltpu.make_async_copy(
        staged_x.at[:, pl.ds(0, half_side), :], cross.at[:, pl.ds(0, half_side), :], f_recv.at[1]
    ).wait()
    wide_packed = lax.broadcasted_iota(jnp.int32, (half_side, side), 0)
    wide_natural = lax.broadcasted_iota(jnp.int32, (half_side, side), 1)
    spread = jnp.where(
        wide_natural == 2 * wide_packed - (wide_packed & (chunk - 1)) + (1 - half) * chunk, 1.0, 0.0
    ).astype(jnp.bfloat16)
    lane = lax.broadcasted_iota(jnp.int32, (chunk, side), 1)
    mine = (lane & chunk) == half * chunk
    for which in range(2):
        turned[...] = facts[which].astype(jnp.float32).T
        for part in range(rows_of):
            own = pl.ds(pl.multiple_of(part * 2 * chunk + half * chunk, chunk), chunk)
            rest = pl.ds(pl.multiple_of(part * 2 * chunk + (1 - half) * chunk, chunk), chunk)
            nf_ref[which, 0, own, :] = facts[which, own, :].astype(jnp.float32)
            far = dot(cross[which, rest, :], spread)
            nf_ref[which, 0, rest, :] = jnp.where(mine, turned[rest, :], far)

    for step in range(1, steps):
        wait_gradients(step)
        add_gram(step)

    eye = (
        lax.broadcasted_iota(jnp.int32, (side, side), 0)
        == lax.broadcasted_iota(jnp.int32, (side, side), 1)
    )
    unit = jnp.where(eye, 1.0, 0.0).astype(jnp.float32)
    for which in range(2):
        stat = nf_ref[which, 0] + acc[which] / side
        nf_ref[which, 0] = stat
        total = jnp.sum(jnp.sum(stat * stat, axis=0, keepdims=True), axis=1, keepdims=True)
        frobenius = jnp.sqrt(total)
        start = 1.0 / jnp.sqrt(jnp.sqrt(frobenius))
        mixer[which] = stat / frobenius
        approx[which] = start * (1.25 * unit - 0.25 * mixer[which])

    def both(left, right):
        return [dot(a, b) for a, b in zip(left, right)]

    for sweep in range(SWITCH):
        m = [mixer[0], mixer[1]]
        square = both(m, m)
        if sweep > 0:
            x = [approx[0], approx[1]]
            step_x = both(x, m)
            for which in range(2):
                approx[which] = 1.25 * x[which] - 0.25 * step_x[which]
        lead = [0.0625 * square[which] - 0.625 * m[which] for which in range(2)]
        inner = [1.5625 * m[which] + part for which, part in enumerate(both(lead, m))]
        for which, part in enumerate(both(lead, inner)):
            grown = 1.5625 * inner[which] + part
            mixer[which] = grown - unit if sweep == SWITCH - 1 else grown
    for sweep in range(SWITCH, ITERS):
        e = [mixer[0], mixer[1]]
        if sweep < ITERS - 1:
            square = both(e, e)
        x = [approx[0], approx[1]]
        step_x = both(x, e)
        for which in range(2):
            approx[which] = x[which] - 0.25 * step_x[which]
        if sweep < ITERS - 1:
            lead = [0.0625 * square[which] - 0.5 * e[which] for which in range(2)]
            inner = [lead[which] + e[which] + part for which, part in enumerate(both(lead, e))]
            for which, part in enumerate(both(lead, inner)):
                mixer[which] = lead[which] + inner[which] + part

    multiplier = scale_ref[layer_ref[slot_ref[me]]]
    applied[...] = dot(approx[0], grads[steps - 1]).astype(jnp.bfloat16)
    right_half = approx[1].astype(jnp.bfloat16)
    band = slab * cols_of
    for turn in range(rows_of):
        target_row = (row + turn) % rows_of
        rows = pl.ds(pl.multiple_of(target_row * band, band), band)
        moved[rows, :] = (multiplier * dot(applied[rows, :], right_half)).astype(jnp.bfloat16)

        def give_back(k, carry):
            target_col = (col + 3 * k) % cols_of
            target = target_row * cols_of + target_col
            pltpu.make_async_remote_copy(
                src_ref=moved.at[strip(target), :],
                dst_ref=returned.at[me],
                send_sem=u_send,
                recv_sem=u_recv,
                device_id=(target_row, target_col),
                device_id_type=MESH,
            ).start()
            return carry

        lax.fori_loop(1 if turn == 0 else 0, cols_of, give_back, 0)
    pltpu.make_async_copy(moved.at[strip(me), :], returned.at[me], u_recv).start()

    most = side - slab
    for step in range(steps):
        sent = staged_g.at[step, pl.ds(0, most), :]
        pltpu.make_async_copy(sent, sent, g_send.at[step]).wait()
    near = staged_f.at[:, pl.ds(0, half_side - slab), :]
    pltpu.make_async_copy(near, near, f_send.at[0]).wait()
    far = staged_x.at[:, pl.ds(0, half_side), :]
    pltpu.make_async_copy(far, far, f_send.at[1]).wait()
    pltpu.make_async_copy(returned, returned, u_recv).wait()

    def unpack(block, carry):
        upd_ref[block] = returned[inverse_ref[block]]
        return carry

    lax.fori_loop(0, blocks, unpack, 0)
    pltpu.make_async_copy(
        moved.at[pl.ds(0, most), :], moved.at[pl.ds(0, most), :], u_send
    ).wait()


def fused_body(rows_of, cols_of, gradients, factors, slot_block, layer_of_block, layer_step_scale):
    steps, blocks, slab, side = gradients.shape
    half_side = side // 2
    in_vmem = pl.BlockSpec(memory_space=pltpu.VMEM)
    in_smem = pl.BlockSpec(memory_space=pltpu.SMEM)
    bf16, f32 = jnp.bfloat16, jnp.float32
    order = jnp.arange(blocks, dtype=jnp.int32)
    inverse = jnp.sum(jnp.where(slot_block[None, :] == order[:, None], order[None, :], 0), axis=1)
    return pl.pallas_call(
        functools.partial(fused_kernel, rows_of, cols_of),
        out_shape=(
            pltpu.VMEM((2, 1, side, side), f32),
            pltpu.VMEM((blocks, slab, side), bf16),
        ),
        in_specs=[in_smem] * 4 + [pl.BlockSpec(memory_space=pl.ANY)] * 2,
        out_specs=(in_vmem, in_vmem),
        scratch_shapes=[
            pltpu.VMEM(gradients.shape, bf16),
            pltpu.VMEM(factors.shape, f32),
            pltpu.VMEM((steps, side, side), bf16),
            pltpu.VMEM((2, side, side), bf16),
            pltpu.VMEM((2, side, half_side), bf16),
            pltpu.VMEM((steps, side, side), bf16),
            pltpu.VMEM((2, side, side), bf16),
            pltpu.VMEM((2, side, half_side), bf16),
            pltpu.VMEM((2, side, side), f32),
            pltpu.VMEM((side, side), f32),
            pltpu.VMEM((2, side, side), f32),
            pltpu.VMEM((2, side, side), f32),
            pltpu.VMEM((side, side), bf16),
            pltpu.VMEM((side, side), bf16),
            pltpu.VMEM((blocks, slab, side), bf16),
            pltpu.SemaphoreType.DMA((steps,)),
            pltpu.SemaphoreType.DMA((steps,)),
            pltpu.SemaphoreType.DMA((2,)),
            pltpu.SemaphoreType.DMA((2,)),
            pltpu.SemaphoreType.DMA,
            pltpu.SemaphoreType.DMA,
            pltpu.SemaphoreType.DMA((2,)),
        ],
        compiler_params=pltpu.CompilerParams(
            collective_id=0, has_side_effects=True, vmem_limit_bytes=56 * 1024 * 1024
        ),
    )(slot_block, inverse, layer_of_block, layer_step_scale, gradients, factors)


def fits(rows_of, cols_of, blocks, slab, side):
    chunk = slab * cols_of // 2
    return (
        blocks == rows_of * cols_of
        and slab % 16 == 0
        and cols_of % 2 == 0
        and cols_of % 3 != 0
        and chunk & (chunk - 1) == 0
        and side % 256 == 0
    )


def solution(mesh):
    rows_of, cols_of = mesh.shape["row"], mesh.shape["col"]

    def body(gradients, factors, *rest):
        _, blocks, slab, side = gradients.shape
        if fits(rows_of, cols_of, blocks, slab, side):
            return fused_body(rows_of, cols_of, gradients, factors, *rest)
        return plain_body(gradients, factors, *rest)

    return jax.shard_map(
        body,
        mesh=mesh,
        in_specs=(
            P(None, None, ("row", "col"), None),
            P(None, None, ("row", "col"), None),
            P(),
            P(),
            P(),
        ),
        out_specs=(P(None, ("row", "col"), None, None), P(None, ("row", "col"), None)),
        check_vma=False,
    )
```

```python
import functools

import jax
import jax.numpy as jnp
from jax import lax
from jax.experimental import pallas as pl
from jax.experimental.pallas import tpu as pltpu
from jax.sharding import PartitionSpec as P

MESH = pl.DeviceIdType.MESH
ITERS = 6
SWITCH = ITERS - 2


def inverse_root(matrix):
    unit_matrix = jnp.eye(matrix.shape[0], dtype=jnp.float32)
    frobenius = jnp.sqrt(jnp.sum(matrix * matrix))
    mixer = matrix / frobenius
    approx = unit_matrix * frobenius ** (-0.25)
    for newton_sweep in range(ITERS):
        factor_p = (5.0 * unit_matrix - mixer) * 0.25
        approx = jnp.dot(approx, factor_p, precision=lax.Precision.HIGHEST)
        second_root_factor = jnp.dot(factor_p, factor_p, precision=lax.Precision.HIGHEST)
        mixer = jnp.dot(
            second_root_factor,
            jnp.dot(second_root_factor, mixer, precision=lax.Precision.HIGHEST),
            precision=lax.Precision.HIGHEST,
        )
    return approx


def plain_body(gradients, factors, slot_block, layer_of_block, layer_step_scale):
    count_steps, block_count, row_slab, block_side = gradients.shape
    row_count = lax.axis_size("row")
    col_count = lax.axis_size("col")
    devices_all = row_count * col_count
    per_device = block_count // devices_all
    ordered_grads = jnp.take(gradients, slot_block, axis=1)
    ordered_factors = jnp.take(factors, slot_block, axis=1)
    owned_grads = lax.all_to_all(
        ordered_grads.reshape(count_steps, block_count, 1, row_slab, block_side),
        ("row", "col"),
        split_axis=1,
        concat_axis=2,
        tiled=True,
    )
    owned_factors = lax.all_to_all(
        ordered_factors.reshape(2, block_count, 1, row_slab, block_side),
        ("row", "col"),
        split_axis=1,
        concat_axis=2,
        tiled=True,
    )
    owned_grads = owned_grads.reshape(count_steps, per_device, block_side, block_side)
    owned_factors = owned_factors.reshape(2, per_device, block_side, block_side)
    first_slot = (lax.axis_index("row") * col_count + lax.axis_index("col")) * per_device
    own_slots = first_slot + jnp.arange(per_device, dtype=jnp.int32)
    own_blocks = jnp.take(slot_block, own_slots)
    own_layers = jnp.take(layer_of_block, own_blocks)
    layer_hits = (
        own_layers[:, None] == jnp.arange(layer_step_scale.shape[0], dtype=jnp.int32)[None, :]
    )
    step_multipliers = jnp.sum(jnp.where(layer_hits, layer_step_scale[None, :], 0.0), axis=1)

    def per_slot(block_position):
        gradient = lax.dynamic_index_in_dim(owned_grads, block_position, 1, keepdims=False)
        held = lax.dynamic_index_in_dim(owned_factors, block_position, 1, keepdims=False)
        gram_left = jnp.einsum(
            "sik,sjk->ij", gradient, gradient, preferred_element_type=jnp.float32
        )
        gram_right = jnp.einsum(
            "ski,skj->ij", gradient, gradient, preferred_element_type=jnp.float32
        )
        left_stat = held[0] + gram_left / block_side
        right_stat = held[1] + gram_right / block_side
        root_left_half = inverse_root(left_stat).astype(jnp.bfloat16)
        root_right_half = inverse_root(right_stat).astype(jnp.bfloat16)
        step_multiplier = lax.dynamic_index_in_dim(
            step_multipliers, block_position, 0, keepdims=False
        )
        left_applied = jnp.dot(
            root_left_half, gradient[count_steps - 1], preferred_element_type=jnp.float32
        ).astype(jnp.bfloat16)
        product = jnp.dot(left_applied, root_right_half, preferred_element_type=jnp.float32)
        return (left_stat, right_stat, (step_multiplier * product).astype(jnp.bfloat16))

    lefts, rights, moved = lax.map(per_slot, jnp.arange(per_device, dtype=jnp.int32))
    new_factors = jnp.stack([lefts, rights])
    returned = lax.all_to_all(
        moved.reshape(1, 1, per_device, devices_all, row_slab, block_side),
        ("row", "col"),
        split_axis=3,
        concat_axis=1,
        tiled=True,
    )
    returned = returned.reshape(block_count, row_slab, block_side)
    update = jnp.zeros_like(returned).at[slot_block].set(returned)
    return (new_factors, update)


def dot(a, b, contract=((1,), (0,))):
    return lax.dot_general(
        a.astype(jnp.bfloat16),
        b.astype(jnp.bfloat16),
        (contract, ((), ())),
        preferred_element_type=jnp.float32,
    )


def fused_kernel(
    rows_of,
    cols_of,
    slot_ref,
    layer_ref,
    scale_ref,
    g_far,
    f_far,
    nf_ref,
    upd_ref,
    g_ref,
    f_ref,
    staged_g,
    staged_f,
    staged_x,
    grads,
    facts,
    cross,
    acc,
    turned,
    mixer,
    approx,
    applied,
    moved,
    returned,
    g_send,
    g_recv,
    f_send,
    f_recv,
    u_send,
    u_recv,
    in_sem,
    inverse_ref,
):
    steps, blocks, slab, side = g_ref.shape
    half_cols = cols_of // 2
    chunk = slab * half_cols
    half_side = side // 2
    row = lax.axis_index("row")
    col = lax.axis_index("col")
    me = row * cols_of + col
    half = col // half_cols
    place = col % half_cols

    def strip(index):
        return pl.ds(pl.multiple_of(index * slab, slab), slab)

    def same_half(k):
        return (row + k // half_cols) % rows_of, half * half_cols + (place + k % half_cols) % half_cols

    def other_half(k):
        return (
            (row + k // half_cols) % rows_of,
            (1 - half) * half_cols + (place + k % half_cols) % half_cols,
        )

    pairs = rows_of * half_cols
    g_fetch = pltpu.make_async_copy(g_far, g_ref, in_sem.at[0])
    f_fetch = pltpu.make_async_copy(f_far, f_ref, in_sem.at[1])
    g_fetch.start()
    f_fetch.start()

    barrier = pltpu.get_barrier_semaphore()

    def greet(k, carry):
        @pl.when(k > 0)
        def _():
            pl.semaphore_signal(barrier, inc=1, device_id=same_half(k), device_id_type=MESH)

        pl.semaphore_signal(barrier, inc=1, device_id=other_half(k), device_id_type=MESH)
        return carry

    lax.fori_loop(0, pairs, greet, 0)

    def stage_gradients(step):
        def one(slot, carry):
            staged_g[step, strip(slot), :] = g_ref[step, slot_ref[slot]]
            return carry

        lax.fori_loop(0, blocks, one, 0, unroll=4)

    g_fetch.wait()
    stage_gradients(0)
    pl.semaphore_wait(barrier, blocks - 1)

    def send_gradients(step):
        def ship(peer):
            target = peer[0] * cols_of + peer[1]
            pltpu.make_async_remote_copy(
                src_ref=staged_g.at[step, strip(target), :],
                dst_ref=grads.at[step, strip(me), :],
                send_sem=g_send.at[step],
                recv_sem=g_recv.at[step],
                device_id=peer,
                device_id_type=MESH,
            ).start()

        def one(k, carry):
            ship(other_half(k))

            @pl.when(k > 0)
            def _():
                ship(same_half(k))

            return carry

        lax.fori_loop(0, pairs, one, 0)
        pltpu.make_async_copy(
            staged_g.at[step, strip(me), :], grads.at[step, strip(me), :], g_recv.at[step]
        ).start()

    send_gradients(0)

    def stage_statistics(slot, carry):
        for which in range(2):
            staged_f[which, strip(slot), :] = f_ref[which, slot_ref[slot]].astype(jnp.bfloat16)
        return carry

    f_fetch.wait()
    lax.fori_loop(0, blocks, stage_statistics, 0, unroll=2)
    natural = lax.broadcasted_iota(jnp.int32, (side, 2 * chunk), 0)
    packed = lax.broadcasted_iota(jnp.int32, (side, 2 * chunk), 1)
    low = packed < chunk
    within = packed & (chunk - 1)
    bands = [((row + ahead) % rows_of) * 2 * chunk + half * chunk for ahead in range(3)]

    def pick(first, second):
        hit = natural == within + jnp.where(low, first, second)
        return jnp.where(hit, 1.0, 0.0).astype(jnp.bfloat16)

    for which in range(2):
        staged_x[which] = dot(staged_f[which], pick(bands[0], bands[1])).astype(jnp.bfloat16)
    staged_x[2] = (
        dot(staged_f[0], pick(bands[2], -side)) + dot(staged_f[1], pick(-side, bands[2]))
    ).astype(jnp.bfloat16)

    def send_statistics(k, carry):
        far = other_half(k)
        pltpu.make_async_remote_copy(
            src_ref=staged_x.at[:, strip(far[0] * cols_of + far[1]), :],
            dst_ref=cross.at[:, strip(me), :],
            send_sem=f_send.at[1],
            recv_sem=f_recv.at[1],
            device_id=far,
            device_id_type=MESH,
        ).start()

        @pl.when(k > 0)
        def _():
            near = same_half(k)
            pltpu.make_async_remote_copy(
                src_ref=staged_f.at[:, strip(near[0] * cols_of + near[1]), :],
                dst_ref=facts.at[:, strip(me), :],
                send_sem=f_send.at[0],
                recv_sem=f_recv.at[0],
                device_id=near,
                device_id_type=MESH,
            ).start()

        return carry

    lax.fori_loop(0, pairs, send_statistics, 0)
    pltpu.make_async_copy(
        staged_f.at[:, strip(me), :], facts.at[:, strip(me), :], f_recv.at[0]
    ).start()
    for step in range(1, steps):
        stage_gradients(step)
        send_gradients(step)

    def find(block, carry):
        found = jnp.int32(0)
        for slot in range(blocks):
            found = found + (slot - found) * (slot_ref[slot] == block).astype(jnp.int32)
        inverse_ref[block] = found
        return carry

    lax.fori_loop(0, blocks, find, 0)

    def wait_gradients(step):
        pltpu.make_async_copy(staged_g.at[step], grads.at[step], g_recv.at[step]).wait()

    def add_gram(step):
        held = grads[step]
        left = dot(held, held, ((1,), (1,)))
        right = dot(held, held, ((0,), (0,)))
        if step == 0:
            acc[0] = left
            acc[1] = right
        else:
            acc[0] += left
            acc[1] += right

    wait_gradients(0)
    add_gram(0)

    pltpu.make_async_copy(
        staged_f.at[:, pl.ds(0, half_side), :], facts.at[:, pl.ds(0, half_side), :], f_recv.at[0]
    ).wait()
    pltpu.make_async_copy(
        staged_x.at[:, pl.ds(0, half_side), :], cross.at[:, pl.ds(0, half_side), :], f_recv.at[1]
    ).wait()
    wide_packed = lax.broadcasted_iota(jnp.int32, (2 * chunk, side), 0)
    wide_natural = lax.broadcasted_iota(jnp.int32, (2 * chunk, side), 1)
    wide_low = wide_packed < chunk
    wide_within = wide_packed & (chunk - 1)

    def spread(first, second):
        hit = wide_natural == wide_within + jnp.where(wide_low, first, second)
        return jnp.where(hit, 1.0, 0.0).astype(jnp.bfloat16)

    def far_band(part):
        return (part % rows_of) * 2 * chunk + (1 - half) * chunk

    lane = lax.broadcasted_iota(jnp.int32, (chunk, side), 1)
    for part in range(rows_of):
        rest = pl.ds(pl.multiple_of(far_band(part), chunk), chunk)
        wide = spread(far_band(part), far_band(part + 1))
        extras = (spread(far_band(part + 2), -side), spread(-side, far_band(part + 2)))
        for which in range(2):
            facts[which, rest, :] = (
                dot(cross[which, rest, :], wide) + dot(cross[2, rest, :], extras[which])
            ).astype(jnp.bfloat16)
    for which in range(2):
        turned[...] = facts[which].astype(jnp.float32).T
        for part in range(rows_of):
            own = pl.ds(pl.multiple_of(part * 2 * chunk + half * chunk, chunk), chunk)
            rest = pl.ds(pl.multiple_of(far_band(part), chunk), chunk)
            mirrored = ((lane & chunk) == half * chunk) | (
                (lane & (side - chunk)) == far_band(part + 3)
            )
            nf_ref[which, 0, own, :] = facts[which, own, :].astype(jnp.float32)
            nf_ref[which, 0, rest, :] = jnp.where(
                mirrored, turned[rest, :], facts[which, rest, :].astype(jnp.float32)
            )

    for step in range(1, steps):
        wait_gradients(step)
        add_gram(step)

    eye = (
        lax.broadcasted_iota(jnp.int32, (side, side), 0)
        == lax.broadcasted_iota(jnp.int32, (side, side), 1)
    )
    unit = jnp.where(eye, 1.0, 0.0).astype(jnp.float32)
    for which in range(2):
        stat = nf_ref[which, 0] + acc[which] / side
        nf_ref[which, 0] = stat
        total = jnp.sum(jnp.sum(stat * stat, axis=0, keepdims=True), axis=1, keepdims=True)
        frobenius = jnp.sqrt(total)
        start = 1.0 / jnp.sqrt(jnp.sqrt(frobenius))
        mixer[which] = stat / frobenius
        approx[which] = start * (1.25 * unit - 0.25 * mixer[which])

    def both(left, right):
        return [dot(a, b) for a, b in zip(left, right)]

    for sweep in range(SWITCH):
        m = [mixer[0], mixer[1]]
        square = both(m, m)
        if sweep > 0:
            x = [approx[0], approx[1]]
            step_x = both(x, m)
            for which in range(2):
                approx[which] = 1.25 * x[which] - 0.25 * step_x[which]
        lead = [0.0625 * square[which] - 0.625 * m[which] for which in range(2)]
        inner = [1.5625 * m[which] + part for which, part in enumerate(both(lead, m))]
        for which, part in enumerate(both(lead, inner)):
            grown = 1.5625 * inner[which] + part
            mixer[which] = grown - unit if sweep == SWITCH - 1 else grown
    e = [mixer[0], mixer[1]]
    x = [approx[0], approx[1]]
    square = both(e, e)
    cube = both(square, e)
    high = [
        0.0341796875 * e[which]
        - 0.004638671875 * square[which]
        + 0.000244140625 * cube[which]
        for which in range(2)
    ]
    shift = [
        0.15625 * square[which] - 0.25 * e[which] - 0.1171875 * cube[which] + part
        for which, part in enumerate(both(cube, high))
    ]
    for which, part in enumerate(both(x, shift)):
        approx[which] = x[which] + part

    multiplier = scale_ref[layer_ref[slot_ref[me]]]
    applied[...] = dot(approx[0], grads[steps - 1]).astype(jnp.bfloat16)
    right_half = approx[1].astype(jnp.bfloat16)
    band = slab * cols_of
    for turn in range(rows_of):
        target_row = (row + turn) % rows_of
        rows = pl.ds(pl.multiple_of(target_row * band, band), band)
        moved[rows, :] = (multiplier * dot(applied[rows, :], right_half)).astype(jnp.bfloat16)

        def give_back(k, carry):
            target_col = (col + 3 * k) % cols_of
            target = target_row * cols_of + target_col
            pltpu.make_async_remote_copy(
                src_ref=moved.at[strip(target), :],
                dst_ref=returned.at[me],
                send_sem=u_send,
                recv_sem=u_recv,
                device_id=(target_row, target_col),
                device_id_type=MESH,
            ).start()
            return carry

        lax.fori_loop(1 if turn == 0 else 0, cols_of, give_back, 0)
    pltpu.make_async_copy(moved.at[strip(me), :], returned.at[me], u_recv).start()

    most = side - slab
    for step in range(steps):
        sent = staged_g.at[step, pl.ds(0, most), :]
        pltpu.make_async_copy(sent, sent, g_send.at[step]).wait()
    near = staged_f.at[:, pl.ds(0, half_side - slab), :]
    pltpu.make_async_copy(near, near, f_send.at[0]).wait()
    far = staged_x.at[:, pl.ds(0, half_side), :]
    pltpu.make_async_copy(far, far, f_send.at[1]).wait()
    pltpu.make_async_copy(returned, returned, u_recv).wait()

    def unpack(block, carry):
        upd_ref[block] = returned[inverse_ref[block]]
        return carry

    lax.fori_loop(0, blocks, unpack, 0)
    pltpu.make_async_copy(
        moved.at[pl.ds(0, most), :], moved.at[pl.ds(0, most), :], u_send
    ).wait()


def fused_body(rows_of, cols_of, gradients, factors, slot_block, layer_of_block, layer_step_scale):
    steps, blocks, slab, side = gradients.shape
    in_vmem = pl.BlockSpec(memory_space=pltpu.VMEM)
    in_smem = pl.BlockSpec(memory_space=pltpu.SMEM)
    bf16, f32 = jnp.bfloat16, jnp.float32
    return pl.pallas_call(
        functools.partial(fused_kernel, rows_of, cols_of),
        out_shape=(
            pltpu.VMEM((2, 1, side, side), f32),
            pltpu.VMEM((blocks, slab, side), bf16),
        ),
        in_specs=[in_smem] * 3 + [pl.BlockSpec(memory_space=pl.ANY)] * 2,
        out_specs=(in_vmem, in_vmem),
        scratch_shapes=[
            pltpu.VMEM(gradients.shape, bf16),
            pltpu.VMEM(factors.shape, f32),
            pltpu.VMEM((steps, side, side), bf16),
            pltpu.VMEM((2, side, side), bf16),
            pltpu.VMEM((3, side, 2 * slab * cols_of // 2), bf16),
            pltpu.VMEM((steps, side, side), bf16),
            pltpu.VMEM((2, side, side), bf16),
            pltpu.VMEM((3, side, 2 * slab * cols_of // 2), bf16),
            pltpu.VMEM((2, side, side), f32),
            pltpu.VMEM((side, side), f32),
            pltpu.VMEM((2, side, side), f32),
            pltpu.VMEM((2, side, side), f32),
            pltpu.VMEM((side, side), bf16),
            pltpu.VMEM((side, side), bf16),
            pltpu.VMEM((blocks, slab, side), bf16),
            pltpu.SemaphoreType.DMA((steps,)),
            pltpu.SemaphoreType.DMA((steps,)),
            pltpu.SemaphoreType.DMA((2,)),
            pltpu.SemaphoreType.DMA((2,)),
            pltpu.SemaphoreType.DMA,
            pltpu.SemaphoreType.DMA,
            pltpu.SemaphoreType.DMA((2,)),
            pltpu.SMEM((blocks,), jnp.int32),
        ],
        compiler_params=pltpu.CompilerParams(
            collective_id=0, has_side_effects=True, vmem_limit_bytes=56 * 1024 * 1024
        ),
    )(slot_block, layer_of_block, layer_step_scale, gradients, factors)


def fits(rows_of, cols_of, blocks, slab, side):
    chunk = slab * cols_of // 2
    return (
        blocks == rows_of * cols_of
        and rows_of == 4
        and 2 * chunk == 128
        and side & (side - 1) == 0
        and slab % 16 == 0
        and cols_of % 2 == 0
        and cols_of % 3 != 0
        and chunk & (chunk - 1) == 0
        and side % 256 == 0
    )


def solution(mesh):
    rows_of, cols_of = mesh.shape["row"], mesh.shape["col"]

    def body(gradients, factors, *rest):
        _, blocks, slab, side = gradients.shape
        if fits(rows_of, cols_of, blocks, slab, side):
            return fused_body(rows_of, cols_of, gradients, factors, *rest)
        return plain_body(gradients, factors, *rest)

    return jax.shard_map(
        body,
        mesh=mesh,
        in_specs=(
            P(None, None, ("row", "col"), None),
            P(None, None, ("row", "col"), None),
            P(),
            P(),
            P(),
        ),
        out_specs=(P(None, ("row", "col"), None, None), P(None, ("row", "col"), None)),
        check_vma=False,
    )
```

```python
import functools

import jax
import jax.numpy as jnp
from jax import lax
from jax.experimental import pallas as pl
from jax.experimental.pallas import tpu as pltpu
from jax.sharding import PartitionSpec as P

MESH = pl.DeviceIdType.MESH
ITERS = 6
SWITCH = ITERS - 2


def inverse_root(matrix):
    unit_matrix = jnp.eye(matrix.shape[0], dtype=jnp.float32)
    frobenius = jnp.sqrt(jnp.sum(matrix * matrix))
    mixer = matrix / frobenius
    approx = unit_matrix * frobenius ** (-0.25)
    for newton_sweep in range(ITERS):
        factor_p = (5.0 * unit_matrix - mixer) * 0.25
        approx = jnp.dot(approx, factor_p, precision=lax.Precision.HIGHEST)
        second_root_factor = jnp.dot(factor_p, factor_p, precision=lax.Precision.HIGHEST)
        mixer = jnp.dot(
            second_root_factor,
            jnp.dot(second_root_factor, mixer, precision=lax.Precision.HIGHEST),
            precision=lax.Precision.HIGHEST,
        )
    return approx


def plain_body(gradients, factors, slot_block, layer_of_block, layer_step_scale):
    count_steps, block_count, row_slab, block_side = gradients.shape
    row_count = lax.axis_size("row")
    col_count = lax.axis_size("col")
    devices_all = row_count * col_count
    per_device = block_count // devices_all
    ordered_grads = jnp.take(gradients, slot_block, axis=1)
    ordered_factors = jnp.take(factors, slot_block, axis=1)
    owned_grads = lax.all_to_all(
        ordered_grads.reshape(count_steps, block_count, 1, row_slab, block_side),
        ("row", "col"),
        split_axis=1,
        concat_axis=2,
        tiled=True,
    )
    owned_factors = lax.all_to_all(
        ordered_factors.reshape(2, block_count, 1, row_slab, block_side),
        ("row", "col"),
        split_axis=1,
        concat_axis=2,
        tiled=True,
    )
    owned_grads = owned_grads.reshape(count_steps, per_device, block_side, block_side)
    owned_factors = owned_factors.reshape(2, per_device, block_side, block_side)
    first_slot = (lax.axis_index("row") * col_count + lax.axis_index("col")) * per_device
    own_slots = first_slot + jnp.arange(per_device, dtype=jnp.int32)
    own_blocks = jnp.take(slot_block, own_slots)
    own_layers = jnp.take(layer_of_block, own_blocks)
    layer_hits = (
        own_layers[:, None] == jnp.arange(layer_step_scale.shape[0], dtype=jnp.int32)[None, :]
    )
    step_multipliers = jnp.sum(jnp.where(layer_hits, layer_step_scale[None, :], 0.0), axis=1)

    def per_slot(block_position):
        gradient = lax.dynamic_index_in_dim(owned_grads, block_position, 1, keepdims=False)
        held = lax.dynamic_index_in_dim(owned_factors, block_position, 1, keepdims=False)
        gram_left = jnp.einsum(
            "sik,sjk->ij", gradient, gradient, preferred_element_type=jnp.float32
        )
        gram_right = jnp.einsum(
            "ski,skj->ij", gradient, gradient, preferred_element_type=jnp.float32
        )
        left_stat = held[0] + gram_left / block_side
        right_stat = held[1] + gram_right / block_side
        root_left_half = inverse_root(left_stat).astype(jnp.bfloat16)
        root_right_half = inverse_root(right_stat).astype(jnp.bfloat16)
        step_multiplier = lax.dynamic_index_in_dim(
            step_multipliers, block_position, 0, keepdims=False
        )
        left_applied = jnp.dot(
            root_left_half, gradient[count_steps - 1], preferred_element_type=jnp.float32
        ).astype(jnp.bfloat16)
        product = jnp.dot(left_applied, root_right_half, preferred_element_type=jnp.float32)
        return (left_stat, right_stat, (step_multiplier * product).astype(jnp.bfloat16))

    lefts, rights, moved = lax.map(per_slot, jnp.arange(per_device, dtype=jnp.int32))
    new_factors = jnp.stack([lefts, rights])
    returned = lax.all_to_all(
        moved.reshape(1, 1, per_device, devices_all, row_slab, block_side),
        ("row", "col"),
        split_axis=3,
        concat_axis=1,
        tiled=True,
    )
    returned = returned.reshape(block_count, row_slab, block_side)
    update = jnp.zeros_like(returned).at[slot_block].set(returned)
    return (new_factors, update)


def dot(a, b, contract=((1,), (0,))):
    return lax.dot_general(
        a.astype(jnp.bfloat16),
        b.astype(jnp.bfloat16),
        (contract, ((), ())),
        preferred_element_type=jnp.float32,
    )


def fused_kernel(
    rows_of,
    cols_of,
    slot_ref,
    layer_ref,
    scale_ref,
    g_far,
    f_far,
    nf_ref,
    upd_ref,
    g_ref,
    f_ref,
    staged_g,
    staged_f,
    staged_x,
    grads,
    facts,
    cross,
    acc,
    turned,
    applied,
    moved,
    returned,
    g_send,
    g_recv,
    f_send,
    f_recv,
    u_send,
    u_recv,
    in_sem,
    inverse_ref,
):
    steps, blocks, slab, side = g_ref.shape
    half_cols = cols_of // 2
    chunk = slab * half_cols
    half_side = side // 2
    row = lax.axis_index("row")
    col = lax.axis_index("col")
    me = row * cols_of + col
    half = col // half_cols
    place = col % half_cols

    def strip(index):
        return pl.ds(pl.multiple_of(index * slab, slab), slab)

    def same_half(k):
        return (row + k // half_cols) % rows_of, half * half_cols + (place + k % half_cols) % half_cols

    def other_half(k):
        return (
            (row + k // half_cols) % rows_of,
            (1 - half) * half_cols + (place + k % half_cols) % half_cols,
        )

    pairs = rows_of * half_cols
    g_fetch = pltpu.make_async_copy(g_far, g_ref, in_sem.at[0])
    f_fetch = pltpu.make_async_copy(f_far, f_ref, in_sem.at[1])
    g_fetch.start()
    f_fetch.start()

    barrier = pltpu.get_barrier_semaphore()

    def greet(k, carry):
        @pl.when(k > 0)
        def _():
            pl.semaphore_signal(barrier, inc=1, device_id=same_half(k), device_id_type=MESH)

        pl.semaphore_signal(barrier, inc=1, device_id=other_half(k), device_id_type=MESH)
        return carry

    lax.fori_loop(0, pairs, greet, 0)

    def stage_gradients(step):
        def one(slot, carry):
            staged_g[step, strip(slot), :] = g_ref[step, slot_ref[slot]]
            return carry

        lax.fori_loop(0, blocks, one, 0, unroll=4)

    g_fetch.wait()
    stage_gradients(0)
    pl.semaphore_wait(barrier, blocks - 1)

    def send_gradients(step):
        def ship(peer):
            target = peer[0] * cols_of + peer[1]
            pltpu.make_async_remote_copy(
                src_ref=staged_g.at[step, strip(target), :],
                dst_ref=grads.at[step, strip(me), :],
                send_sem=g_send.at[step],
                recv_sem=g_recv.at[step],
                device_id=peer,
                device_id_type=MESH,
            ).start()

        def one(k, carry):
            ship(other_half(k))

            @pl.when(k > 0)
            def _():
                ship(same_half(k))

            return carry

        lax.fori_loop(0, pairs, one, 0)
        pltpu.make_async_copy(
            staged_g.at[step, strip(me), :], grads.at[step, strip(me), :], g_recv.at[step]
        ).start()

    send_gradients(0)

    def stage_statistics(slot, carry):
        for which in range(2):
            staged_f[which, strip(slot), :] = f_ref[which, slot_ref[slot]].astype(jnp.bfloat16)
        return carry

    f_fetch.wait()
    lax.fori_loop(0, blocks, stage_statistics, 0, unroll=2)
    natural = lax.broadcasted_iota(jnp.int32, (side, 2 * chunk), 0)
    packed = lax.broadcasted_iota(jnp.int32, (side, 2 * chunk), 1)
    low = packed < chunk
    within = packed & (chunk - 1)
    bands = [((row + ahead) % rows_of) * 2 * chunk + half * chunk for ahead in range(3)]

    def pick(first, second):
        hit = natural == within + jnp.where(low, first, second)
        return jnp.where(hit, 1.0, 0.0).astype(jnp.bfloat16)

    for which in range(2):
        staged_x[which] = dot(staged_f[which], pick(bands[0], bands[1])).astype(jnp.bfloat16)
    staged_x[2] = (
        dot(staged_f[0], pick(bands[2], -side)) + dot(staged_f[1], pick(-side, bands[2]))
    ).astype(jnp.bfloat16)

    def send_statistics(k, carry):
        far = other_half(k)
        pltpu.make_async_remote_copy(
            src_ref=staged_x.at[:, strip(far[0] * cols_of + far[1]), :],
            dst_ref=cross.at[:, strip(me), :],
            send_sem=f_send.at[1],
            recv_sem=f_recv.at[1],
            device_id=far,
            device_id_type=MESH,
        ).start()

        @pl.when(k > 0)
        def _():
            near = same_half(k)
            pltpu.make_async_remote_copy(
                src_ref=staged_f.at[:, strip(near[0] * cols_of + near[1]), :],
                dst_ref=facts.at[:, strip(me), :],
                send_sem=f_send.at[0],
                recv_sem=f_recv.at[0],
                device_id=near,
                device_id_type=MESH,
            ).start()

        return carry

    lax.fori_loop(0, pairs, send_statistics, 0)
    pltpu.make_async_copy(
        staged_f.at[:, strip(me), :], facts.at[:, strip(me), :], f_recv.at[0]
    ).start()
    for step in range(1, steps):
        stage_gradients(step)
        send_gradients(step)

    def find(block, carry):
        found = jnp.int32(0)
        for slot in range(blocks):
            found = found + (slot - found) * (slot_ref[slot] == block).astype(jnp.int32)
        inverse_ref[block] = found
        return carry

    lax.fori_loop(0, blocks, find, 0)

    def wait_gradients(step):
        pltpu.make_async_copy(staged_g.at[step], grads.at[step], g_recv.at[step]).wait()

    def add_gram(step):
        held = grads[step]
        left = dot(held, held, ((1,), (1,)))
        right = dot(held, held, ((0,), (0,)))
        if step == 0:
            acc[0] = left
            acc[1] = right
        else:
            acc[0] += left
            acc[1] += right

    wait_gradients(0)
    add_gram(0)

    pltpu.make_async_copy(
        staged_f.at[:, pl.ds(0, half_side), :], facts.at[:, pl.ds(0, half_side), :], f_recv.at[0]
    ).wait()
    pltpu.make_async_copy(
        staged_x.at[:, pl.ds(0, half_side), :], cross.at[:, pl.ds(0, half_side), :], f_recv.at[1]
    ).wait()
    wide_packed = lax.broadcasted_iota(jnp.int32, (2 * chunk, side), 0)
    wide_natural = lax.broadcasted_iota(jnp.int32, (2 * chunk, side), 1)
    wide_low = wide_packed < chunk
    wide_within = wide_packed & (chunk - 1)

    def spread(first, second):
        hit = wide_natural == wide_within + jnp.where(wide_low, first, second)
        return jnp.where(hit, 1.0, 0.0).astype(jnp.bfloat16)

    def far_band(part):
        return (part % rows_of) * 2 * chunk + (1 - half) * chunk

    lane = lax.broadcasted_iota(jnp.int32, (chunk, side), 1)
    for part in range(rows_of):
        rest = pl.ds(pl.multiple_of(far_band(part), chunk), chunk)
        wide = spread(far_band(part), far_band(part + 1))
        extras = (spread(far_band(part + 2), -side), spread(-side, far_band(part + 2)))
        for which in range(2):
            facts[which, rest, :] = (
                dot(cross[which, rest, :], wide) + dot(cross[2, rest, :], extras[which])
            ).astype(jnp.bfloat16)
    for which in range(2):
        turned[...] = facts[which].astype(jnp.float32).T
        for part in range(rows_of):
            own = pl.ds(pl.multiple_of(part * 2 * chunk + half * chunk, chunk), chunk)
            rest = pl.ds(pl.multiple_of(far_band(part), chunk), chunk)
            mirrored = ((lane & chunk) == half * chunk) | (
                (lane & (side - chunk)) == far_band(part + 3)
            )
            nf_ref[which, 0, own, :] = facts[which, own, :].astype(jnp.float32)
            nf_ref[which, 0, rest, :] = jnp.where(
                mirrored, turned[rest, :], facts[which, rest, :].astype(jnp.float32)
            )

    for step in range(1, steps):
        wait_gradients(step)
        add_gram(step)

    hs = side // 2

    def unit_of(shape):
        hit = lax.broadcasted_iota(jnp.int32, shape, 0) == lax.broadcasted_iota(jnp.int32, shape, 1)
        return jnp.where(hit, 1.0, 0.0).astype(jnp.float32)

    unit = (unit_of((hs, side)), unit_of((hs, hs)))

    def per_part(form, *matrices):
        return tuple(form(*parts) for parts in zip(*matrices))

    def operand(matrix):
        upper, corner = matrix
        lower = jnp.concatenate([upper[:, hs:].T, corner], axis=1)
        return jnp.concatenate([upper.astype(jnp.bfloat16), lower.astype(jnp.bfloat16)], axis=0)

    def operands(matrices):
        return [operand(matrix) for matrix in matrices]

    def both(left, right):
        return [(dot(p[:hs], q), dot(p[hs:], q[:, hs:])) for p, q in zip(left, right)]

    sides = range(2)
    m, x = [], []
    for which in sides:
        stat = nf_ref[which, 0] + acc[which] / side
        nf_ref[which, 0] = stat
        total = jnp.sum(jnp.sum(stat * stat, axis=0, keepdims=True), axis=1, keepdims=True)
        frobenius = jnp.sqrt(total)
        start = 1.0 / jnp.sqrt(jnp.sqrt(frobenius))
        scaled = (stat[:hs] / frobenius, stat[hs:, hs:] / frobenius)
        m.append(scaled)
        x.append(per_part(lambda u, v: start * (1.25 * u - 0.25 * v), unit, scaled))

    for sweep in range(SWITCH):
        m_op = operands(m)
        square = both(m_op, m_op)
        if sweep > 0:
            step_x = both(operands(x), m_op)
            x = [per_part(lambda u, v: 1.25 * u - 0.25 * v, x[w], step_x[w]) for w in sides]
        lead = operands(
            [per_part(lambda u, v: 0.0625 * u - 0.625 * v, square[w], m[w]) for w in sides]
        )
        product = both(lead, m_op)
        inner = [per_part(lambda u, v: 1.5625 * u + v, m[w], product[w]) for w in sides]
        product = both(lead, operands(inner))
        m = [per_part(lambda u, v: 1.5625 * u + v, inner[w], product[w]) for w in sides]

    e = [per_part(lambda u, v: u - v, m[w], unit) for w in sides]
    e_op = operands(e)
    square = both(e_op, e_op)
    cube = both(operands(square), e_op)
    high = operands(
        [
            per_part(
                lambda u, v, w: 0.0341796875 * u - 0.004638671875 * v + 0.000244140625 * w,
                e[w],
                square[w],
                cube[w],
            )
            for w in sides
        ]
    )
    product = both(operands(cube), high)
    shift = operands(
        [
            per_part(
                lambda u, v, w, t: 0.15625 * v - 0.25 * u - 0.1171875 * w + t,
                e[w],
                square[w],
                cube[w],
                product[w],
            )
            for w in sides
        ]
    )
    product = both(operands(x), shift)
    left_half, right_half = operands(
        [per_part(lambda u, v: u + v, x[w], product[w]) for w in sides]
    )

    multiplier = scale_ref[layer_ref[slot_ref[me]]]
    applied[...] = dot(left_half, grads[steps - 1]).astype(jnp.bfloat16)
    band = slab * cols_of
    for turn in range(rows_of):
        target_row = (row + turn) % rows_of
        rows = pl.ds(pl.multiple_of(target_row * band, band), band)
        moved[rows, :] = (multiplier * dot(applied[rows, :], right_half)).astype(jnp.bfloat16)

        def give_back(k, carry):
            target_col = (col + 3 * k) % cols_of
            target = target_row * cols_of + target_col
            pltpu.make_async_remote_copy(
                src_ref=moved.at[strip(target), :],
                dst_ref=returned.at[me],
                send_sem=u_send,
                recv_sem=u_recv,
                device_id=(target_row, target_col),
                device_id_type=MESH,
            ).start()
            return carry

        lax.fori_loop(1 if turn == 0 else 0, cols_of, give_back, 0)
    pltpu.make_async_copy(moved.at[strip(me), :], returned.at[me], u_recv).start()

    most = side - slab
    for step in range(steps):
        sent = staged_g.at[step, pl.ds(0, most), :]
        pltpu.make_async_copy(sent, sent, g_send.at[step]).wait()
    near = staged_f.at[:, pl.ds(0, half_side - slab), :]
    pltpu.make_async_copy(near, near, f_send.at[0]).wait()
    far = staged_x.at[:, pl.ds(0, half_side), :]
    pltpu.make_async_copy(far, far, f_send.at[1]).wait()
    pltpu.make_async_copy(returned, returned, u_recv).wait()

    def unpack(block, carry):
        upd_ref[block] = returned[inverse_ref[block]]
        return carry

    lax.fori_loop(0, blocks, unpack, 0)
    pltpu.make_async_copy(
        moved.at[pl.ds(0, most), :], moved.at[pl.ds(0, most), :], u_send
    ).wait()


def fused_body(rows_of, cols_of, gradients, factors, slot_block, layer_of_block, layer_step_scale):
    steps, blocks, slab, side = gradients.shape
    in_vmem = pl.BlockSpec(memory_space=pltpu.VMEM)
    in_smem = pl.BlockSpec(memory_space=pltpu.SMEM)
    bf16, f32 = jnp.bfloat16, jnp.float32
    return pl.pallas_call(
        functools.partial(fused_kernel, rows_of, cols_of),
        out_shape=(
            pltpu.VMEM((2, 1, side, side), f32),
            pltpu.VMEM((blocks, slab, side), bf16),
        ),
        in_specs=[in_smem] * 3 + [pl.BlockSpec(memory_space=pl.ANY)] * 2,
        out_specs=(in_vmem, in_vmem),
        scratch_shapes=[
            pltpu.VMEM(gradients.shape, bf16),
            pltpu.VMEM(factors.shape, f32),
            pltpu.VMEM((steps, side, side), bf16),
            pltpu.VMEM((2, side, side), bf16),
            pltpu.VMEM((3, side, 2 * slab * cols_of // 2), bf16),
            pltpu.VMEM((steps, side, side), bf16),
            pltpu.VMEM((2, side, side), bf16),
            pltpu.VMEM((3, side, 2 * slab * cols_of // 2), bf16),
            pltpu.VMEM((2, side, side), f32),
            pltpu.VMEM((side, side), f32),
            pltpu.VMEM((side, side), bf16),
            pltpu.VMEM((side, side), bf16),
            pltpu.VMEM((blocks, slab, side), bf16),
            pltpu.SemaphoreType.DMA((steps,)),
            pltpu.SemaphoreType.DMA((steps,)),
            pltpu.SemaphoreType.DMA((2,)),
            pltpu.SemaphoreType.DMA((2,)),
            pltpu.SemaphoreType.DMA,
            pltpu.SemaphoreType.DMA,
            pltpu.SemaphoreType.DMA((2,)),
            pltpu.SMEM((blocks,), jnp.int32),
        ],
        compiler_params=pltpu.CompilerParams(
            collective_id=0, has_side_effects=True, vmem_limit_bytes=56 * 1024 * 1024
        ),
    )(slot_block, layer_of_block, layer_step_scale, gradients, factors)


def fits(rows_of, cols_of, blocks, slab, side):
    chunk = slab * cols_of // 2
    return (
        blocks == rows_of * cols_of
        and rows_of == 4
        and 2 * chunk == 128
        and side & (side - 1) == 0
        and slab % 16 == 0
        and cols_of % 2 == 0
        and cols_of % 3 != 0
        and chunk & (chunk - 1) == 0
        and side % 256 == 0
    )


def solution(mesh):
    rows_of, cols_of = mesh.shape["row"], mesh.shape["col"]

    def body(gradients, factors, *rest):
        _, blocks, slab, side = gradients.shape
        if fits(rows_of, cols_of, blocks, slab, side):
            return fused_body(rows_of, cols_of, gradients, factors, *rest)
        return plain_body(gradients, factors, *rest)

    return jax.shard_map(
        body,
        mesh=mesh,
        in_specs=(
            P(None, None, ("row", "col"), None),
            P(None, None, ("row", "col"), None),
            P(),
            P(),
            P(),
        ),
        out_specs=(P(None, ("row", "col"), None, None), P(None, ("row", "col"), None)),
        check_vma=False,
    )
```

```python
import functools

import jax
import jax.numpy as jnp
from jax import lax
from jax.experimental import pallas as pl
from jax.experimental.pallas import tpu as pltpu
from jax.sharding import PartitionSpec as P

MESH = pl.DeviceIdType.MESH
ITERS = 6
SWITCH = ITERS - 2


def inverse_root(matrix):
    unit_matrix = jnp.eye(matrix.shape[0], dtype=jnp.float32)
    frobenius = jnp.sqrt(jnp.sum(matrix * matrix))
    mixer = matrix / frobenius
    approx = unit_matrix * frobenius ** (-0.25)
    for newton_sweep in range(ITERS):
        factor_p = (5.0 * unit_matrix - mixer) * 0.25
        approx = jnp.dot(approx, factor_p, precision=lax.Precision.HIGHEST)
        second_root_factor = jnp.dot(factor_p, factor_p, precision=lax.Precision.HIGHEST)
        mixer = jnp.dot(
            second_root_factor,
            jnp.dot(second_root_factor, mixer, precision=lax.Precision.HIGHEST),
            precision=lax.Precision.HIGHEST,
        )
    return approx


def plain_body(gradients, factors, slot_block, layer_of_block, layer_step_scale):
    count_steps, block_count, row_slab, block_side = gradients.shape
    row_count = lax.axis_size("row")
    col_count = lax.axis_size("col")
    devices_all = row_count * col_count
    per_device = block_count // devices_all
    ordered_grads = jnp.take(gradients, slot_block, axis=1)
    ordered_factors = jnp.take(factors, slot_block, axis=1)
    owned_grads = lax.all_to_all(
        ordered_grads.reshape(count_steps, block_count, 1, row_slab, block_side),
        ("row", "col"),
        split_axis=1,
        concat_axis=2,
        tiled=True,
    )
    owned_factors = lax.all_to_all(
        ordered_factors.reshape(2, block_count, 1, row_slab, block_side),
        ("row", "col"),
        split_axis=1,
        concat_axis=2,
        tiled=True,
    )
    owned_grads = owned_grads.reshape(count_steps, per_device, block_side, block_side)
    owned_factors = owned_factors.reshape(2, per_device, block_side, block_side)
    first_slot = (lax.axis_index("row") * col_count + lax.axis_index("col")) * per_device
    own_slots = first_slot + jnp.arange(per_device, dtype=jnp.int32)
    own_blocks = jnp.take(slot_block, own_slots)
    own_layers = jnp.take(layer_of_block, own_blocks)
    layer_hits = (
        own_layers[:, None] == jnp.arange(layer_step_scale.shape[0], dtype=jnp.int32)[None, :]
    )
    step_multipliers = jnp.sum(jnp.where(layer_hits, layer_step_scale[None, :], 0.0), axis=1)

    def per_slot(block_position):
        gradient = lax.dynamic_index_in_dim(owned_grads, block_position, 1, keepdims=False)
        held = lax.dynamic_index_in_dim(owned_factors, block_position, 1, keepdims=False)
        gram_left = jnp.einsum(
            "sik,sjk->ij", gradient, gradient, preferred_element_type=jnp.float32
        )
        gram_right = jnp.einsum(
            "ski,skj->ij", gradient, gradient, preferred_element_type=jnp.float32
        )
        left_stat = held[0] + gram_left / block_side
        right_stat = held[1] + gram_right / block_side
        root_left_half = inverse_root(left_stat).astype(jnp.bfloat16)
        root_right_half = inverse_root(right_stat).astype(jnp.bfloat16)
        step_multiplier = lax.dynamic_index_in_dim(
            step_multipliers, block_position, 0, keepdims=False
        )
        left_applied = jnp.dot(
            root_left_half, gradient[count_steps - 1], preferred_element_type=jnp.float32
        ).astype(jnp.bfloat16)
        product = jnp.dot(left_applied, root_right_half, preferred_element_type=jnp.float32)
        return (left_stat, right_stat, (step_multiplier * product).astype(jnp.bfloat16))

    lefts, rights, moved = lax.map(per_slot, jnp.arange(per_device, dtype=jnp.int32))
    new_factors = jnp.stack([lefts, rights])
    returned = lax.all_to_all(
        moved.reshape(1, 1, per_device, devices_all, row_slab, block_side),
        ("row", "col"),
        split_axis=3,
        concat_axis=1,
        tiled=True,
    )
    returned = returned.reshape(block_count, row_slab, block_side)
    update = jnp.zeros_like(returned).at[slot_block].set(returned)
    return (new_factors, update)


def dot(a, b, contract=((1,), (0,))):
    return lax.dot_general(
        a.astype(jnp.bfloat16),
        b.astype(jnp.bfloat16),
        (contract, ((), ())),
        preferred_element_type=jnp.float32,
    )


def fused_kernel(
    rows_of,
    cols_of,
    slot_ref,
    layer_ref,
    scale_ref,
    g_far,
    f_far,
    nf_ref,
    upd_ref,
    g_ref,
    f_ref,
    staged_g,
    staged_f,
    staged_x,
    grads,
    facts,
    cross,
    acc,
    turned,
    applied,
    moved,
    returned,
    g_send,
    g_recv,
    f_send,
    f_recv,
    u_send,
    u_recv,
    in_sem,
    inverse_ref,
):
    steps, blocks, slab, side = g_ref.shape
    half_cols = cols_of // 2
    chunk = slab * half_cols
    half_side = side // 2
    row = lax.axis_index("row")
    col = lax.axis_index("col")
    me = row * cols_of + col
    half = col // half_cols
    place = col % half_cols

    def strip(index):
        return pl.ds(pl.multiple_of(index * slab, slab), slab)

    def same_half(k):
        return (row + k // half_cols) % rows_of, half * half_cols + (place + k % half_cols) % half_cols

    def other_half(k):
        return (
            (row + k // half_cols) % rows_of,
            (1 - half) * half_cols + (place + k % half_cols) % half_cols,
        )

    pairs = rows_of * half_cols
    g_fetch = pltpu.make_async_copy(g_far, g_ref, in_sem.at[0])
    f_fetch = pltpu.make_async_copy(f_far, f_ref, in_sem.at[1])
    g_fetch.start()
    f_fetch.start()

    barrier = pltpu.get_barrier_semaphore()

    for k in range(pairs):
        if k > 0:
            pl.semaphore_signal(barrier, inc=1, device_id=same_half(k), device_id_type=MESH)
        pl.semaphore_signal(barrier, inc=1, device_id=other_half(k), device_id_type=MESH)

    def stage_gradients(step):
        def one(slot, carry):
            staged_g[step, strip(slot), :] = g_ref[step, slot_ref[slot]]
            return carry

        lax.fori_loop(0, blocks, one, 0, unroll=4)

    g_fetch.wait()
    stage_gradients(0)
    pl.semaphore_wait(barrier, blocks - 1)

    def send_gradients(step):
        def ship(peer):
            target = peer[0] * cols_of + peer[1]
            pltpu.make_async_remote_copy(
                src_ref=staged_g.at[step, strip(target), :],
                dst_ref=grads.at[step, strip(me), :],
                send_sem=g_send.at[step],
                recv_sem=g_recv.at[step],
                device_id=peer,
                device_id_type=MESH,
            ).start()

        def one(k, carry):
            ship(other_half(k))

            @pl.when(k > 0)
            def _():
                ship(same_half(k))

            return carry

        lax.fori_loop(0, pairs, one, 0)
        pltpu.make_async_copy(
            staged_g.at[step, strip(me), :], grads.at[step, strip(me), :], g_recv.at[step]
        ).start()

    send_gradients(0)

    def stage_statistics(slot, carry):
        for which in range(2):
            staged_f[which, strip(slot), :] = f_ref[which, slot_ref[slot]].astype(jnp.bfloat16)
        return carry

    f_fetch.wait()
    lax.fori_loop(0, blocks, stage_statistics, 0, unroll=2)
    natural = lax.broadcasted_iota(jnp.int32, (side, 2 * chunk), 0)
    packed = lax.broadcasted_iota(jnp.int32, (side, 2 * chunk), 1)
    low = packed < chunk
    within = packed & (chunk - 1)
    bands = [((row + ahead) % rows_of) * 2 * chunk + half * chunk for ahead in range(3)]

    def pick(first, second):
        hit = natural == within + jnp.where(low, first, second)
        return jnp.where(hit, 1.0, 0.0).astype(jnp.bfloat16)

    for which in range(2):
        staged_x[which] = dot(staged_f[which], pick(bands[0], bands[1])).astype(jnp.bfloat16)
    staged_x[2] = (
        dot(staged_f[0], pick(bands[2], -side)) + dot(staged_f[1], pick(-side, bands[2]))
    ).astype(jnp.bfloat16)

    def send_statistics(k, carry):
        far = other_half(k)
        pltpu.make_async_remote_copy(
            src_ref=staged_x.at[:, strip(far[0] * cols_of + far[1]), :],
            dst_ref=cross.at[:, strip(me), :],
            send_sem=f_send.at[1],
            recv_sem=f_recv.at[1],
            device_id=far,
            device_id_type=MESH,
        ).start()

        @pl.when(k > 0)
        def _():
            near = same_half(k)
            pltpu.make_async_remote_copy(
                src_ref=staged_f.at[:, strip(near[0] * cols_of + near[1]), :],
                dst_ref=facts.at[:, strip(me), :],
                send_sem=f_send.at[0],
                recv_sem=f_recv.at[0],
                device_id=near,
                device_id_type=MESH,
            ).start()

        return carry

    lax.fori_loop(0, pairs, send_statistics, 0)
    pltpu.make_async_copy(
        staged_f.at[:, strip(me), :], facts.at[:, strip(me), :], f_recv.at[0]
    ).start()
    for step in range(1, steps):
        stage_gradients(step)
        send_gradients(step)

    def find(block, carry):
        found = jnp.int32(0)
        for slot in range(blocks):
            found = found + (slot - found) * (slot_ref[slot] == block).astype(jnp.int32)
        inverse_ref[block] = found
        return carry

    lax.fori_loop(0, blocks, find, 0)

    def wait_gradients(step):
        pltpu.make_async_copy(staged_g.at[step], grads.at[step], g_recv.at[step]).wait()

    def add_gram(step):
        held = grads[step]
        left = dot(held, held, ((1,), (1,)))
        right = dot(held, held, ((0,), (0,)))
        if step == 0:
            acc[0] = left
            acc[1] = right
        else:
            acc[0] += left
            acc[1] += right

    wait_gradients(0)
    add_gram(0)

    pltpu.make_async_copy(
        staged_f.at[:, pl.ds(0, half_side), :], facts.at[:, pl.ds(0, half_side), :], f_recv.at[0]
    ).wait()
    pltpu.make_async_copy(
        staged_x.at[:, pl.ds(0, half_side), :], cross.at[:, pl.ds(0, half_side), :], f_recv.at[1]
    ).wait()
    wide_packed = lax.broadcasted_iota(jnp.int32, (2 * chunk, side), 0)
    wide_natural = lax.broadcasted_iota(jnp.int32, (2 * chunk, side), 1)
    wide_low = wide_packed < chunk
    wide_within = wide_packed & (chunk - 1)

    def spread(first, second):
        hit = wide_natural == wide_within + jnp.where(wide_low, first, second)
        return jnp.where(hit, 1.0, 0.0).astype(jnp.bfloat16)

    def far_band(part):
        return (part % rows_of) * 2 * chunk + (1 - half) * chunk

    lane = lax.broadcasted_iota(jnp.int32, (chunk, side), 1)
    for part in range(rows_of):
        rest = pl.ds(pl.multiple_of(far_band(part), chunk), chunk)
        wide = spread(far_band(part), far_band(part + 1))
        extras = (spread(far_band(part + 2), -side), spread(-side, far_band(part + 2)))
        for which in range(2):
            facts[which, rest, :] = (
                dot(cross[which, rest, :], wide) + dot(cross[2, rest, :], extras[which])
            ).astype(jnp.bfloat16)
    for which in range(2):
        turned[...] = facts[which].astype(jnp.float32).T
        for part in range(rows_of):
            own = pl.ds(pl.multiple_of(part * 2 * chunk + half * chunk, chunk), chunk)
            rest = pl.ds(pl.multiple_of(far_band(part), chunk), chunk)
            mirrored = ((lane & chunk) == half * chunk) | (
                (lane & (side - chunk)) == far_band(part + 3)
            )
            nf_ref[which, 0, own, :] = facts[which, own, :].astype(jnp.float32)
            nf_ref[which, 0, rest, :] = jnp.where(
                mirrored, turned[rest, :], facts[which, rest, :].astype(jnp.float32)
            )

    for step in range(1, steps - 1):
        wait_gradients(step)
        add_gram(step)
    scale_back = 1.0 / side
    for which in range(2):
        nf_ref[which, 0] += acc[which] * scale_back
    hs = side // 2
    wait_gradients(steps - 1)
    last = grads[steps - 1]
    grams = (
        (
            dot(last[:hs], last, ((1,), (1,))),
            dot(last[hs:], last[hs:], ((1,), (1,))),
        ),
        (
            dot(last[:, :hs], last, ((0,), (0,))),
            dot(last[:, hs:], last[:, hs:], ((0,), (0,))),
        ),
    )


    def unit_of(shape):
        hit = lax.broadcasted_iota(jnp.int32, shape, 0) == lax.broadcasted_iota(jnp.int32, shape, 1)
        return jnp.where(hit, 1.0, 0.0).astype(jnp.float32)

    unit = (unit_of((hs, side)), unit_of((hs, hs)))

    def per_part(form, *matrices):
        return tuple(form(*parts) for parts in zip(*matrices))

    def operand(matrix):
        upper, corner = matrix
        lower = jnp.concatenate([upper[:, hs:].T, corner], axis=1)
        return jnp.concatenate([upper.astype(jnp.bfloat16), lower.astype(jnp.bfloat16)], axis=0)

    def operands(matrices):
        return [operand(matrix) for matrix in matrices]

    def both(left, right):
        return [(dot(p[:hs], q), dot(p[hs:], q[:, hs:])) for p, q in zip(left, right)]

    sides = range(2)
    m, x = [], []
    for which in sides:
        upper = nf_ref[which, 0, pl.ds(0, hs), :] + grams[which][0] * scale_back
        corner = nf_ref[which, 0, pl.ds(hs, hs), pl.ds(hs, hs)] + grams[which][1] * scale_back
        nf_ref[which, 0, pl.ds(0, hs), :] = upper
        nf_ref[which, 0, pl.ds(hs, hs), pl.ds(0, hs)] = upper[:, hs:].T
        nf_ref[which, 0, pl.ds(hs, hs), pl.ds(hs, hs)] = corner
        across = upper[:, hs:]
        squares = upper[:, :hs] * upper[:, :hs] + 2.0 * (across * across) + corner * corner
        total = jnp.sum(jnp.sum(squares, axis=0, keepdims=True), axis=1, keepdims=True)
        frobenius = jnp.sqrt(total)
        start = 1.0 / jnp.sqrt(jnp.sqrt(frobenius))
        shrink = 1.0 / frobenius
        scaled = (upper * shrink, corner * shrink)
        m.append(scaled)
        x.append(per_part(lambda u, v: start * (1.25 * u - 0.25 * v), unit, scaled))

    for sweep in range(SWITCH):
        m_op = operands(m)
        square = both(m_op, m_op)
        if sweep > 0:
            step_x = both(operands(x), m_op)
            x = [per_part(lambda u, v: 1.25 * u - 0.25 * v, x[w], step_x[w]) for w in sides]
        lead = operands(
            [per_part(lambda u, v: 0.0625 * u - 0.625 * v, square[w], m[w]) for w in sides]
        )
        product = both(lead, m_op)
        inner = [per_part(lambda u, v: 1.5625 * u + v, m[w], product[w]) for w in sides]
        product = both(lead, operands(inner))
        m = [per_part(lambda u, v: 1.5625 * u + v, inner[w], product[w]) for w in sides]

    e = [per_part(lambda u, v: u - v, m[w], unit) for w in sides]
    e_op = operands(e)
    square = both(e_op, e_op)
    cube = both(operands(square), e_op)
    high = operands(
        [
            per_part(
                lambda u, v, w: 0.0341796875 * u - 0.004638671875 * v + 0.000244140625 * w,
                e[w],
                square[w],
                cube[w],
            )
            for w in sides
        ]
    )
    product = both(operands(cube), high)
    shift = operands(
        [
            per_part(
                lambda u, v, w, t: 0.15625 * v - 0.25 * u - 0.1171875 * w + t,
                e[w],
                square[w],
                cube[w],
                product[w],
            )
            for w in sides
        ]
    )
    product = both(operands(x), shift)
    left_half, right_half = operands(
        [per_part(lambda u, v: u + v, x[w], product[w]) for w in sides]
    )

    multiplier = scale_ref[layer_ref[slot_ref[me]]]
    applied[...] = dot(left_half, grads[steps - 1]).astype(jnp.bfloat16)
    band = slab * cols_of
    for turn in range(rows_of):
        target_row = (row + turn) % rows_of
        rows = pl.ds(pl.multiple_of(target_row * band, band), band)
        moved[rows, :] = (multiplier * dot(applied[rows, :], right_half)).astype(jnp.bfloat16)

        def give_back(k, carry):
            target_col = (col + 3 * k) % cols_of
            target = target_row * cols_of + target_col
            pltpu.make_async_remote_copy(
                src_ref=moved.at[strip(target), :],
                dst_ref=returned.at[me],
                send_sem=u_send,
                recv_sem=u_recv,
                device_id=(target_row, target_col),
                device_id_type=MESH,
            ).start()
            return carry

        lax.fori_loop(1 if turn == 0 else 0, cols_of, give_back, 0)
    pltpu.make_async_copy(moved.at[strip(me), :], returned.at[me], u_recv).start()

    most = side - slab
    for step in range(steps):
        sent = staged_g.at[step, pl.ds(0, most), :]
        pltpu.make_async_copy(sent, sent, g_send.at[step]).wait()
    near = staged_f.at[:, pl.ds(0, half_side - slab), :]
    pltpu.make_async_copy(near, near, f_send.at[0]).wait()
    far = staged_x.at[:, pl.ds(0, half_side), :]
    pltpu.make_async_copy(far, far, f_send.at[1]).wait()
    pltpu.make_async_copy(returned, returned, u_recv).wait()

    def unpack(block, carry):
        upd_ref[block] = returned[inverse_ref[block]]
        return carry

    lax.fori_loop(0, blocks, unpack, 0, unroll=8)
    pltpu.make_async_copy(
        moved.at[pl.ds(0, most), :], moved.at[pl.ds(0, most), :], u_send
    ).wait()


def fused_body(rows_of, cols_of, gradients, factors, slot_block, layer_of_block, layer_step_scale):
    steps, blocks, slab, side = gradients.shape
    in_vmem = pl.BlockSpec(memory_space=pltpu.VMEM)
    in_smem = pl.BlockSpec(memory_space=pltpu.SMEM)
    bf16, f32 = jnp.bfloat16, jnp.float32
    return pl.pallas_call(
        functools.partial(fused_kernel, rows_of, cols_of),
        out_shape=(
            pltpu.VMEM((2, 1, side, side), f32),
            pltpu.VMEM((blocks, slab, side), bf16),
        ),
        in_specs=[in_smem] * 3 + [pl.BlockSpec(memory_space=pl.ANY)] * 2,
        out_specs=(in_vmem, in_vmem),
        scratch_shapes=[
            pltpu.VMEM(gradients.shape, bf16),
            pltpu.VMEM(factors.shape, f32),
            pltpu.VMEM((steps, side, side), bf16),
            pltpu.VMEM((2, side, side), bf16),
            pltpu.VMEM((3, side, 2 * slab * cols_of // 2), bf16),
            pltpu.VMEM((steps, side, side), bf16),
            pltpu.VMEM((2, side, side), bf16),
            pltpu.VMEM((3, side, 2 * slab * cols_of // 2), bf16),
            pltpu.VMEM((2, side, side), f32),
            pltpu.VMEM((side, side), f32),
            pltpu.VMEM((side, side), bf16),
            pltpu.VMEM((side, side), bf16),
            pltpu.VMEM((blocks, slab, side), bf16),
            pltpu.SemaphoreType.DMA((steps,)),
            pltpu.SemaphoreType.DMA((steps,)),
            pltpu.SemaphoreType.DMA((2,)),
            pltpu.SemaphoreType.DMA((2,)),
            pltpu.SemaphoreType.DMA,
            pltpu.SemaphoreType.DMA,
            pltpu.SemaphoreType.DMA((2,)),
            pltpu.SMEM((blocks,), jnp.int32),
        ],
        compiler_params=pltpu.CompilerParams(
            collective_id=0, has_side_effects=True, vmem_limit_bytes=56 * 1024 * 1024
        ),
    )(slot_block, layer_of_block, layer_step_scale, gradients, factors)


def fits(rows_of, cols_of, blocks, slab, side):
    chunk = slab * cols_of // 2
    return (
        blocks == rows_of * cols_of
        and rows_of == 4
        and 2 * chunk == 128
        and side & (side - 1) == 0
        and slab % 16 == 0
        and cols_of % 2 == 0
        and cols_of % 3 != 0
        and chunk & (chunk - 1) == 0
        and side % 256 == 0
    )


def solution(mesh):
    rows_of, cols_of = mesh.shape["row"], mesh.shape["col"]

    def body(gradients, factors, *rest):
        _, blocks, slab, side = gradients.shape
        if fits(rows_of, cols_of, blocks, slab, side):
            return fused_body(rows_of, cols_of, gradients, factors, *rest)
        return plain_body(gradients, factors, *rest)

    return jax.shard_map(
        body,
        mesh=mesh,
        in_specs=(
            P(None, None, ("row", "col"), None),
            P(None, None, ("row", "col"), None),
            P(),
            P(),
            P(),
        ),
        out_specs=(P(None, ("row", "col"), None, None), P(None, ("row", "col"), None)),
        check_vma=False,
    )
```
